32 devices in a mesh: ctx: 8 (over z, x), qg: 4 (over y, core).
Axes of the slice: x: 2, y: 2, z: 4, core: 2. Of those that a mesh axis runs over, the one named last changes fastest.
Arguments:
- queries: bfloat16 [16, 32, 768], P('qg'), may hold values from -9 to 9
- documents: bfloat16 [8, 4096, 768], P('qg', 'ctx'), may hold values from -2.5 to 2.5
- candidates: int32 [16, 4], replicated, may hold values from 0 to 7, all different within a row
Outputs:
- loss: float32 [], replicated
- grad_queries: bfloat16 [16, 32, 768], P('qg')
- grad_documents: bfloat16 [8, 4096, 768], P('qg', 'ctx')
The draws below stay inside these ranges and needn't reach their ends.
Inputs may be any that keep to these rules, and one draw needn't show every extreme that they name: `candidates`: each row names 4 different documents; every document is named by some row.
All inputs are finite; a program needn't handle non-finite values.
Results may differ from the reference program's by a relative error of at most 0.006.
Values may be sent and summed in bfloat16 or wider, within the bound.
A program may use at most 64 MiB of HBM per device.

```python
import jax
import jax.numpy as jnp
from jax import lax

MODEL_WIDTH = 768
QT = 32
CANDIDATE_DOCS = 4
L = 4096
QUERY_COUNT = 16
ND = 8


def draw_queries(key, part):
    base = jnp.clip(jax.random.normal(jax.random.fold_in(key, 11), (QUERY_COUNT, QT, MODEL_WIDTH), jnp.float32), -6.0, 6.0) * MODEL_WIDTH ** (-0.25)
    return base.astype(jnp.bfloat16)


def draw_documents(key, part):
    base = jnp.clip(jax.random.normal(jax.random.fold_in(key, 21), (ND, L, MODEL_WIDTH), jnp.float32), -6.0, 6.0) * MODEL_WIDTH ** (-0.25)
    return base.astype(jnp.bfloat16)


def choose_distinct(key, rows, count, top, lift):
    sequence = jax.random.permutation(jax.random.fold_in(key, 1), count)
    boost = sequence
    for power in range(3):
        boost = boost * boost // count
    boost = boost * lift // count
    tickets = jax.random.randint(jax.random.fold_in(key, 2), (rows, count), 0, 4096) + boost
    holders = jax.random.permutation(jax.random.fold_in(key, 3), rows)[jnp.arange(count) % rows]
    tickets = jnp.where(jnp.arange(rows)[:, None] == holders[None, :], 1 << 14, tickets)
    merit = tickets * count + jnp.arange(count)
    return lax.top_k(merit.astype(jnp.int32), top)[1].astype(jnp.int32)


def setup_inputs(seed: int = 0) -> dict:
    arg_keys = jax.random.split(jax.random.key(seed), 4)
    return {
        "queries": draw_queries(jax.random.fold_in(arg_keys[3], 71), 0),
        "documents": draw_documents(jax.random.fold_in(arg_keys[3], 71), 0),
        "candidates": choose_distinct(arg_keys[2], QUERY_COUNT, ND, CANDIDATE_DOCS, 8192),
    }


sharpness_factor = 2.0
loss_scale = 1024.0


def reference(queries, documents, candidates):
    query_ids = jnp.repeat(jnp.arange(QUERY_COUNT, dtype=jnp.int32), CANDIDATE_DOCS)
    doc_ids = candidates.reshape(-1).astype(jnp.int32)

    def forward(pair_ids):
        query_index, document_index = pair_ids
        candidate_logits = sharpness_factor * lax.dot_general(queries[query_index], documents[document_index], (((1,), (1,)), ((), ())), preferred_element_type=jnp.float32)
        return candidate_logits, jax.nn.logsumexp(candidate_logits, axis=1)

    logits_all, log_partition = lax.map(forward, (query_ids, doc_ids))
    query_document_pair = (jnp.sum(log_partition, axis=1) / sharpness_factor).reshape(QUERY_COUNT, CANDIDATE_DOCS)
    total = jax.nn.logsumexp(query_document_pair, axis=1)
    loss = jnp.mean(total - query_document_pair[:, 0])
    first = (jnp.arange(CANDIDATE_DOCS) == 0).astype(jnp.float32)
    dz = (loss_scale / QUERY_COUNT) * (jnp.exp(query_document_pair - total[:, None]) - first[None, :])

    def backward(carry, item):
        grad_q, grad_d = carry
        query_index, document_index, candidate_logits, norm, weight = item
        weighted = (weight * jnp.exp(candidate_logits - norm[:, None])).astype(jnp.bfloat16)
        grad_q = grad_q.at[query_index].add(jnp.dot(weighted, documents[document_index], preferred_element_type=jnp.float32))
        grad_d = grad_d.at[document_index].add(lax.dot_general(weighted, queries[query_index], (((0,), (0,)), ((), ())), preferred_element_type=jnp.float32))
        return (grad_q, grad_d), None

    start = (jnp.zeros((QUERY_COUNT, QT, MODEL_WIDTH), jnp.float32), jnp.zeros((ND, L, MODEL_WIDTH), jnp.float32))
    (grad_q, grad_d), unused = lax.scan(backward, start, (query_ids, doc_ids, logits_all, log_partition, dz.reshape(-1)))
    return loss, grad_q.astype(jnp.bfloat16), grad_d.astype(jnp.bfloat16)
```

```python
import functools

import jax
import jax.numpy as jnp
from jax import lax
from jax.experimental import pallas as pl
from jax.experimental.pallas import tpu as pltpu
from jax.sharding import PartitionSpec as P

sharpness_factor = 2.0
loss_scale = 1024.0
MESH = pl.DeviceIdType.MESH
f32 = jnp.float32
bf16 = jnp.bfloat16


def each(lo, hi, f):
    if hi - lo <= 16:
        for k in range(lo, hi):
            f(k)
    else:
        pl.loop(lo, hi)(f)


def when(always, cond, f):
    if always:
        f()
    else:
        pl.when(cond)(f)


def wrap(i, n):
    return lax.rem(i + 2 * n, n)


def kernel(
    C, NQ, qlen,
    cand, q_ref, d_hbm,
    loss_ref, gq_ref, gd_hbm,
    Q, D, E, G, M, L, Lr, T, S, SC, As, Ar, Bs, Br, Mine, Cs, Cr, Fs, Fr, gd,
    d_sem, gd_sem, qs, qr, fs, ls, lr, ts, tr, a_s, a_r, b_s, b_r, c_s, c_r, f_s, f_r,
):
    nd, tok, width = D.shape
    rows = q_ref.shape[0]
    Y = NQ // 2
    nq = rows // qlen
    slots = cand.shape[1]
    rpc = Cr.shape[1]
    nred = rows // rpc
    full = nred == C
    c = lax.axis_index("ctx")
    g = lax.axis_index("qg")
    y = g // 2
    core = lax.rem(g, 2)
    sib = 2 * y + 1 - core

    def rc(src, dst, ssem, rsem, cc, gg):
        return pltpu.make_async_remote_copy(
            src_ref=src, dst_ref=dst, send_sem=ssem, recv_sem=rsem,
            device_id=(cc, gg), device_id_type=MESH,
        )

    dcopy = [pltpu.make_async_copy(d_hbm.at[d], D.at[d], d_sem.at[d]) for d in range(nd)]
    for x in dcopy:
        x.start()

    barrier = pltpu.get_barrier_semaphore()
    for k in range(1, NQ):
        pl.semaphore_signal(barrier, inc=1, device_id=(c, wrap(g + k, NQ)), device_id_type=MESH)
    each(1, C, lambda k: pl.semaphore_signal(
        barrier, inc=1, device_id=(wrap(c + k, C), g), device_id_type=MESH))
    pl.semaphore_wait(barrier, NQ - 1 + C - 1)

    def q_to_y(k):
        return rc(q_ref, Q.at[g], qs.at[k], qr.at[g], c, wrap(g + 2 * k, NQ))

    q_to_sib = rc(q_ref, Q.at[g], qs.at[0], qr.at[g], c, sib)
    for k in range(1, Y):
        q_to_y(k).start()
    q_to_sib.start()
    Q[g] = q_ref[...]

    lane_q = lax.broadcasted_iota(jnp.int32, (NQ, rows), 1) // qlen
    sub_g = lax.broadcasted_iota(jnp.int32, (NQ, rows), 0)
    qid = sub_g * nq + lane_q
    ids = []
    for k in range(slots):
        v = jnp.zeros((NQ, rows), jnp.int32)
        for q in range(cand.shape[0]):
            v = jnp.where(qid == q, cand[q, k], v)
        ids.append(v)

    def wait_q(src):
        rc(q_ref, Q.at[src], qs.at[0], qr.at[src], c, sib).wait_recv()

    def fwd(yb):
        qb = Q[pl.ds(2 * yb, 2)].reshape(2 * rows, width)
        for d in range(nd):
            lg = sharpness_factor * lax.dot_general(
                D[d], qb, (((1,), (1,)), ((), ())), preferred_element_type=f32)
            m = jnp.max(lg, axis=0, keepdims=True)
            e = jnp.exp(lg - m)
            E[yb, d] = e
            lp = m + jnp.log(jnp.sum(e, axis=0, keepdims=True))
            for h in range(2):
                r = pl.ds(d * NQ + 2 * yb + h, 1)
                M[r, :] = m[:, h * rows:(h + 1) * rows]
                L[r, :] = lp[:, h * rows:(h + 1) * rows]

    def gmat(yb):
        for d in range(nd):
            p = lax.dot_general(
                E[yb, d].astype(bf16), D[d], (((0,), (0,)), ((), ())), preferred_element_type=f32)
            G[d, pl.ds(2 * yb, 2)] = p.reshape(2, rows, width)

    wait_q(sib)
    for x in dcopy:
        x.wait()
    fwd(y)
    gmat(y)
    fwd_copies = []
    for k in range(1, Y):
        src = wrap(g - 2 * k, NQ)
        wait_q(src)
        cp = rc(Q.at[src], Q.at[src], fs.at[k], qr.at[src], c, sib)
        cp.start()
        fwd_copies.append(cp)
    for k in range(1, Y):
        wait_q(wrap(sib - 2 * k, NQ))
        fwd(wrap(y - k, Y))

    def l_copy(k):
        return rc(L, Lr.at[k], ls.at[k], lr.at[k], wrap(c + k, C), g)

    each(1, C, lambda k: l_copy(k).start())
    for k in range(1, Y):
        gmat(wrap(y - k, Y))
    Lr[0] = L[...]
    each(1, C, lambda k: l_copy(k).wait_recv())
    parts = Lr[...]
    top = jnp.max(parts, axis=0)
    lse = top + jnp.log(jnp.sum(jnp.exp(parts - top[None]), axis=0))

    lane = lax.broadcasted_iota(jnp.int32, lse.shape, 1)
    seg = lse
    step = 1
    while step < qlen:
        seg = seg + pltpu.roll(seg, step, 1)
        step *= 2
    seg = jnp.where(lax.rem(lane, qlen) == qlen - 1, seg, 0.0)
    step = 1
    while step < qlen:
        seg = seg + pltpu.roll(seg, rows - step, 1)
        step *= 2
    T[g] = seg / sharpness_factor

    def t_copy(k):
        return rc(T.at[g], T.at[g], ts.at[k], tr.at[k], c, wrap(g + k, NQ))

    for k in range(1, NQ):
        t_copy(k).start()
    shrink = jnp.exp(M[...] - lse)
    for k in range(1, NQ):
        src = wrap(g - k, NQ)
        rc(T.at[src], T.at[src], ts.at[k], tr.at[k], c, src).wait_recv()

    pairs = []
    for k in range(slots):
        v = jnp.zeros((NQ, rows), f32)
        for gg in range(NQ):
            for d in range(nd):
                v = jnp.where(ids[k] == gg * nd + d, T[gg, d * NQ:(d + 1) * NQ, :], v)
        pairs.append(v)
    highest = functools.reduce(jnp.maximum, pairs)
    total = highest + jnp.log(functools.reduce(jnp.add, [jnp.exp(p - highest) for p in pairs]))
    loss_ref[0, 0] = jnp.sum(total - pairs[0]) / (NQ * rows)
    dz = [
        loss_scale / (NQ * nq) * (jnp.exp(p - total) - (1.0 if k == 0 else 0.0))
        for k, p in enumerate(pairs)
    ]
    for d in range(nd):
        w = jnp.zeros((NQ, rows), f32)
        for k in range(slots):
            w = w + jnp.where(ids[k] == g * nd + d, dz[k], 0.0)
        S[d * NQ:(d + 1) * NQ, :] = w * shrink[d * NQ:(d + 1) * NQ, :]
    St = jnp.transpose(S[...])
    for gg in range(NQ):
        for d in range(nd):
            r = d * NQ + gg
            SC[gg, d] = jnp.broadcast_to(St[:, r:r + 1], (rows, 128))

    def scaled(gg, lo):
        v = SC[gg, 0] * G[0, gg, :, lo:lo + 128]
        for d in range(1, nd):
            v = v + SC[gg, d] * G[d, gg, :, lo:lo + 128]
        return v

    cols = range(0, width, 128)

    def a_copy(yy):
        return rc(As.at[yy], Ar.at[yy], a_s.at[yy], a_r.at[yy], c, sib)

    for k in range(1, Y + 1):
        yy = wrap(y + k, Y)
        for lo in cols:
            As[yy, :, lo:lo + 128] = scaled(2 * yy + 1 - core, lo).astype(bf16)
        a_copy(yy).start()

    def b_copy(k):
        return rc(Bs.at[k], Br.at[k], b_s.at[k], b_r.at[k], c, wrap(g + 2 * k, NQ))

    for k in range(1, Y):
        yy = wrap(y + k, Y)
        a_copy(yy).wait_recv()
        for lo in cols:
            Bs[k, :, lo:lo + 128] = (
                scaled(2 * yy + core, lo) + Ar[yy, :, lo:lo + 128].astype(f32)).astype(bf16)
        b_copy(k).start()
    a_copy(y).wait_recv()
    for lo in cols:
        Mine[:, lo:lo + 128] = scaled(g, lo) + Ar[y, :, lo:lo + 128].astype(f32)

    for d in range(nd):
        acc = None
        for yb in range(Y):
            r = d * NQ + 2 * yb
            s = jnp.concatenate([S[r:r + 1, :], S[r + 1:r + 2, :]], axis=1)
            wt = (E[yb, d] * s).astype(bf16)
            part = jnp.dot(wt, Q[2 * yb:2 * yb + 2].reshape(2 * rows, width),
                           preferred_element_type=f32)
            acc = part if acc is None else acc + part
        gd[d] = acc.astype(bf16)
        pltpu.make_async_copy(gd.at[d], gd_hbm.at[d], gd_sem.at[d]).start()

    for k in range(1, Y):
        b_copy(k).wait_recv()
        Mine[...] = Mine[...] + Br[k].astype(f32)
    Cs[...] = Mine[...].astype(bf16).reshape(nred, rpc, width)

    def c_copy(k):
        to = wrap(c + k, C)
        return to, rc(Cs.at[lax.rem(to, nred)], Cr.at[k], c_s.at[k], c_r.at[k], to, g)

    def c_start(k):
        to, cp = c_copy(k)
        when(full, to < nred, cp.start)

    each(1, C, c_start)
    mine_c = c < nred

    def reduce_share():
        each(1, C, lambda k: c_copy(k)[1].wait_recv())
        at = pl.multiple_of(lax.rem(c, nred) * rpc, rpc)
        Cr[0] = jnp.zeros((rpc, width), bf16)
        v = Mine[pl.ds(at, rpc), :] + jnp.sum(Cr[...].astype(f32), axis=0)
        Fs[...] = v.astype(bf16)
        each(1, C, lambda k: rc(
            Fs, Fr.at[lax.rem(c, nred)], f_s.at[k], f_r.at[k], wrap(c + k, C), g).start())
        Fr[lax.rem(c, nred)] = Fs[...]

    when(full, mine_c, reduce_share)

    def f_wait(k):
        src = wrap(c - k, C)
        cp = rc(Fs, Fr.at[lax.rem(src, nred)], f_s.at[k], f_r.at[k], src, g)
        when(full, src < nred, cp.wait_recv)

    each(1, C, f_wait)
    gq_ref[...] = Fr[...].reshape(rows, width)

    for k in range(1, Y):
        q_to_y(k).wait_send()
    q_to_sib.wait_send()
    for cp in fwd_copies:
        cp.wait_send()
    each(1, C, lambda k: l_copy(k).wait_send())
    for k in range(1, NQ):
        t_copy(k).wait_send()
    for yy in range(Y):
        a_copy(yy).wait_send()
    for k in range(1, Y):
        b_copy(k).wait_send()

    def c_done(k):
        to, cp = c_copy(k)
        when(full, to < nred, cp.wait_send)

    each(1, C, c_done)
    when(full, mine_c, lambda: each(1, C, lambda k: rc(
        Fs, Fr.at[lax.rem(c, nred)], f_s.at[k], f_r.at[k], wrap(c + k, C), g).wait_send()))
    for d in range(nd):
        pltpu.make_async_copy(gd.at[d], gd_hbm.at[d], gd_sem.at[d]).wait()


def per_device(C, NQ, queries, documents, candidates):
    nq, qlen, width = queries.shape
    nd, tok, _ = documents.shape
    rows = nq * qlen
    Y = NQ // 2
    rpc = max(16, rows // C)
    nred = rows // rpc
    dma = pltpu.SemaphoreType.DMA
    V = pltpu.VMEM
    loss, gq, gd = pl.pallas_call(
        functools.partial(kernel, C, NQ, qlen),
        out_shape=(
            jax.ShapeDtypeStruct((1, 1), f32),
            jax.ShapeDtypeStruct((rows, width), bf16),
            jax.ShapeDtypeStruct((nd, tok, width), bf16),
        ),
        in_specs=[
            pl.BlockSpec(memory_space=pltpu.SMEM),
            pl.BlockSpec(memory_space=pltpu.VMEM),
            pl.BlockSpec(memory_space=pl.ANY),
        ],
        out_specs=(
            pl.BlockSpec(memory_space=pltpu.SMEM),
            pl.BlockSpec(memory_space=pltpu.VMEM),
            pl.BlockSpec(memory_space=pl.ANY),
        ),
        scratch_shapes=[
            V((NQ, rows, width), bf16),
            V((nd, tok, width), bf16),
            V((Y, nd, tok, 2 * rows), f32),
            V((nd, NQ, rows, width), f32),
            V((nd * NQ, rows), f32),
            V((nd * NQ, rows), f32),
            V((C, nd * NQ, rows), f32),
            V((NQ, nd * NQ, rows), f32),
            V((nd * NQ, rows), f32),
            V((NQ, nd, rows, 128), f32),
            V((Y, rows, width), bf16),
            V((Y, rows, width), bf16),
            V((Y, rows, width), bf16),
            V((Y, rows, width), bf16),
            V((rows, width), f32),
            V((nred, rpc, width), bf16),
            V((C, rpc, width), bf16),
            V((rpc, width), bf16),
            V((nred, rpc, width), bf16),
            V((nd, tok, width), bf16),
            dma((nd,)), dma((nd,)),
            dma((Y,)), dma((NQ,)), dma((Y,)),
            dma((C,)), dma((C,)),
            dma((NQ,)), dma((NQ,)),
            dma((Y,)), dma((Y,)),
            dma((Y,)), dma((Y,)),
            dma((C,)), dma((C,)),
            dma((C,)), dma((C,)),
        ],
        compiler_params=pltpu.CompilerParams(
            collective_id=0, has_side_effects=True, vmem_limit_bytes=48 * 1024 * 1024),
    )(candidates, queries.reshape(rows, width), documents)
    return loss.reshape(()), gq.reshape(nq, qlen, width), gd


def solution(mesh):
    return jax.shard_map(
        functools.partial(per_device, mesh.shape["ctx"], mesh.shape["qg"]),
        mesh=mesh,
        in_specs=(P("qg", None, None), P("qg", "ctx", None), P()),
        out_specs=(P(), P("qg", None, None), P("qg", "ctx", None)),
        check_vma=False,
    )
```

```python
import functools

import jax
import jax.numpy as jnp
from jax import lax
from jax.experimental import pallas as pl
from jax.experimental.pallas import tpu as pltpu
from jax.sharding import PartitionSpec as P

sharpness_factor = 2.0
loss_scale = 1024.0
MESH = pl.DeviceIdType.MESH
f32 = jnp.float32
bf16 = jnp.bfloat16


def each(lo, hi, f):
    if hi - lo <= 16:
        for k in range(lo, hi):
            f(k)
    else:
        pl.loop(lo, hi)(f)


def when(always, cond, f):
    if always:
        f()
    else:
        pl.when(cond)(f)


def wrap(i, n):
    return lax.rem(i + 2 * n, n)


def kernel(
    C, NQ, qlen,
    cand, q_hbm, d_hbm,
    loss_ref, gq_ref, gd_hbm,
    Q, D, E, G, M, L, Lr, T, S, Sh, Shr, Ss, SC, As, Ar, Bs, Br, Mine, Cs, Cr, Fs, Fr, gd,
    d_sem, gd_sem, ql, qs, qr, fs, ls, lr, ts, tr, sh_sem, a_s, a_r, b_s, b_r, c_s, c_r, f_s, f_r,
):
    nd, tok, width = D.shape
    rows = Q.shape[1]
    Y = NQ // 2
    nq = rows // qlen
    slots = cand.shape[0]
    NC = Mine.shape[0]
    cw = width // NC
    rpc = Cr.shape[2]
    nred = rows // rpc
    full = nred == C
    c = lax.axis_index("ctx")
    g = lax.axis_index("qg")
    y = g // 2
    core = lax.rem(g, 2)
    sib = 2 * y + 1 - core

    def rc(src, dst, ssem, rsem, cc, gg):
        return pltpu.make_async_remote_copy(
            src_ref=src, dst_ref=dst, send_sem=ssem, recv_sem=rsem,
            device_id=(cc, gg), device_id_type=MESH,
        )

    barrier = pltpu.get_barrier_semaphore()
    for k in range(1, NQ):
        pl.semaphore_signal(barrier, inc=1, device_id=(c, wrap(g + k, NQ)), device_id_type=MESH)
    each(1, C, lambda k: pl.semaphore_signal(
        barrier, inc=1, device_id=(wrap(c + k, C), g), device_id_type=MESH))
    q_own = pltpu.make_async_copy(q_hbm, Q.at[g], ql)
    q_own.start()
    dcopy = [pltpu.make_async_copy(d_hbm.at[d], D.at[d], d_sem.at[d]) for d in range(nd)]
    for x in dcopy:
        x.start()
    pl.semaphore_wait(barrier, NQ - 1 + C - 1)

    def q_to_y(k):
        return rc(q_hbm, Q.at[g], qs.at[k], qr.at[g], c, wrap(g + 2 * k, NQ))

    q_to_sib = rc(q_hbm, Q.at[g], qs.at[0], qr.at[g], c, sib)
    for k in range(1, Y):
        q_to_y(k).start()
    q_to_sib.start()

    lane_q = lax.broadcasted_iota(jnp.int32, (NQ, rows), 1) // qlen
    sub_g = lax.broadcasted_iota(jnp.int32, (NQ, rows), 0)
    qid = sub_g * nq + lane_q
    ids = []
    for k in range(slots):
        v = jnp.zeros((NQ, rows), jnp.int32)
        for q in range(cand.shape[1]):
            v = jnp.where(qid == q, cand[k, q], v)
        ids.append(v)

    def wait_q(src):
        rc(q_hbm, Q.at[src], qs.at[0], qr.at[src], c, sib).wait_recv()

    def fwd(first, n):
        qb = Q[pl.ds(first, n)].reshape(n * rows, width)
        for d in range(nd):
            lg = sharpness_factor * lax.dot_general(
                D[d], qb, (((1,), (1,)), ((), ())), preferred_element_type=f32)
            m = jnp.max(lg, axis=0, keepdims=True)
            e = jnp.exp(lg - m)
            lp = m + jnp.log(jnp.sum(e, axis=0, keepdims=True))
            for h in range(n):
                r = pl.ds(d * NQ + first + h, 1)
                E[first + h, d] = e[:, h * rows:(h + 1) * rows]
                M[r, :] = m[:, h * rows:(h + 1) * rows]
                L[r, :] = lp[:, h * rows:(h + 1) * rows]

    def a_copy(yb):
        return rc(As.at[yb], Ar.at[yb], a_s.at[yb], a_r.at[yb], c, sib)

    def gmat(yb):
        for d in range(nd):
            e = jnp.concatenate([E[2 * yb, d].astype(bf16), E[2 * yb + 1, d].astype(bf16)], axis=1)
            p = lax.dot_general(
                e, D[d], (((0,), (0,)), ((), ())), preferred_element_type=f32)
            G[d, pl.ds(2 * yb, 2)] = p.reshape(2, rows, width)
            As[yb, d] = G[d, 2 * yb + 1 - core].astype(bf16)
        a_copy(yb).start()

    q_own.wait()
    wait_q(sib)
    for x in dcopy:
        x.wait()
    fwd(2 * y, 2)
    gmat(y)
    fwd_copies = []
    for k in range(1, Y):
        src = wrap(g - 2 * k, NQ)
        wait_q(src)
        cp = rc(Q.at[src], Q.at[src], fs.at[k], qr.at[src], c, sib)
        cp.start()
        fwd_copies.append(cp)
        fwd(src, 1)
    for k in range(1, Y):
        src = wrap(sib - 2 * k, NQ)
        wait_q(src)
        fwd(src, 1)

    def l_copy(k):
        return rc(L, Lr.at[k], ls.at[k], lr.at[k], wrap(c + k, C), g)

    each(1, C, lambda k: l_copy(k).start())
    for k in range(1, Y):
        gmat(wrap(y - k, Y))
    Lr[0] = L[...]
    each(1, C, lambda k: l_copy(k).wait_recv())
    parts = Lr[...]
    top = jnp.max(parts, axis=0)
    lse = top + jnp.log(jnp.sum(jnp.exp(parts - top[None]), axis=0))

    lane = lax.broadcasted_iota(jnp.int32, lse.shape, 1)
    seg = lse
    step = 1
    while step < qlen:
        seg = seg + pltpu.roll(seg, step, 1)
        step *= 2
    seg = jnp.where(lax.rem(lane, qlen) == qlen - 1, seg, 0.0)
    step = 1
    while step < qlen:
        seg = seg + pltpu.roll(seg, rows - step, 1)
        step *= 2
    T[g] = seg / sharpness_factor

    def t_copy(k):
        return rc(T.at[g], T.at[g], ts.at[k], tr.at[k], c, wrap(g + k, NQ))

    for k in range(1, NQ):
        t_copy(k).start()
    Sh[...] = jnp.exp(M[...] - lse)
    sh_copy = rc(Sh, Shr, sh_sem.at[0], sh_sem.at[1], c, sib)
    sh_copy.start()
    for k in range(1, NQ):
        src = wrap(g - k, NQ)
        rc(T.at[src], T.at[src], ts.at[k], tr.at[k], c, src).wait_recv()

    pairs = []
    for k in range(slots):
        v = jnp.zeros((NQ, rows), f32)
        for gg in range(NQ):
            for d in range(nd):
                v = jnp.where(ids[k] == gg * nd + d, T[gg, d * NQ:(d + 1) * NQ, :], v)
        pairs.append(v)
    highest = functools.reduce(jnp.maximum, pairs)
    total = highest + jnp.log(functools.reduce(jnp.add, [jnp.exp(p - highest) for p in pairs]))
    loss_ref[0, 0] = jnp.sum(total - pairs[0]) / (NQ * rows)
    dz = [
        loss_scale / (NQ * nq) * (jnp.exp(p - total) - (1.0 if k == 0 else 0.0))
        for k, p in enumerate(pairs)
    ]
    sh_copy.wait_recv()
    for d in range(nd):
        r = slice(d * NQ, (d + 1) * NQ)
        for grp, shrink, dst in ((g, Sh, S), (sib, Shr, Ss)):
            w = jnp.zeros((NQ, rows), f32)
            for k in range(slots):
                w = w + jnp.where(ids[k] == grp * nd + d, dz[k], 0.0)
            dst[r, :] = w * shrink[r, :]
    own = [
        src[pl.ds(d * NQ + 2 * yy + core, 1), :]
        for yy in range(Y) for src in (S, Ss) for d in range(nd)
    ]
    St = jnp.transpose(jnp.concatenate(own, axis=0))
    for i in range(len(own)):
        SC[i // (2 * nd), i % (2 * nd)] = jnp.broadcast_to(St[:, i:i + 1], (rows, 128))

    for k in range(Y):
        a_copy(wrap(y - k, Y)).wait_recv()

    def scaled(yy, lo):
        at = slice(lo, lo + 128)
        v = SC[yy, 0] * G[0, 2 * yy + core, :, at]
        for d in range(1, nd):
            v = v + SC[yy, d] * G[d, 2 * yy + core, :, at]
        for d in range(nd):
            v = v + SC[yy, nd + d] * Ar[yy, d, :, at].astype(f32)
        return v

    def b_copy(n, k):
        return rc(Bs.at[n, k], Br.at[n, k], b_s.at[n, k], b_r.at[n, k], c, wrap(g + 2 * k, NQ))

    for n in range(NC):
        for k in range(1, Y):
            for lo in range(0, cw, 128):
                Bs[n, k, :, lo:lo + 128] = scaled(wrap(y + k, Y), n * cw + lo).astype(bf16)
            b_copy(n, k).start()
    for n in range(NC):
        for lo in range(0, cw, 128):
            Mine[n, :, lo:lo + 128] = scaled(y, n * cw + lo)

    for d in range(nd):
        acc = None
        for yb in range(Y):
            r = d * NQ + 2 * yb
            wt = jnp.concatenate(
                [(E[2 * yb + h, d] * S[r + h:r + h + 1, :]).astype(bf16) for h in range(2)], axis=1)
            part = jnp.dot(wt, Q[2 * yb:2 * yb + 2].reshape(2 * rows, width),
                           preferred_element_type=f32)
            acc = part if acc is None else acc + part
        gd[d] = acc.astype(bf16)
        pltpu.make_async_copy(gd.at[d], gd_hbm.at[d], gd_sem.at[d]).start()

    share = lax.rem(c, nred)

    def c_copy(n, k):
        to = wrap(c + k, C)
        return to, rc(
            Cs.at[n, lax.rem(to, nred)], Cr.at[n, k], c_s.at[n, k], c_r.at[n, k], to, g)

    def f_copy(n, k):
        return rc(Fs.at[n], Fr.at[n, share], f_s.at[n, k], f_r.at[n, k], wrap(c + k, C), g)

    for n in range(NC):
        for k in range(1, Y):
            b_copy(n, k).wait_recv()
            Mine[n] = Mine[n] + Br[n, k].astype(f32)
        Cs[n] = Mine[n].astype(bf16).reshape(nred, rpc, cw)

        def c_start(k, n=n):
            to, cp = c_copy(n, k)
            when(full, to < nred, cp.start)

        each(1, C, c_start)

    for n in range(NC):
        def reduce_share(n=n):
            at = pl.multiple_of(share * rpc, rpc)
            Cr[n, 0] = jnp.zeros((rpc, cw), bf16)
            each(1, C, lambda k: c_copy(n, k)[1].wait_recv())
            v = Mine[n, pl.ds(at, rpc), :] + jnp.sum(Cr[n].astype(f32), axis=0)
            Fs[n] = v.astype(bf16)
            each(1, C, lambda k: f_copy(n, k).start())
            Fr[n, share] = Fs[n]

        when(full, c < nred, reduce_share)

    for n in range(NC):
        def f_wait(k, n=n):
            src = wrap(c - k, C)
            cp = rc(Fs.at[n], Fr.at[n, lax.rem(src, nred)], f_s.at[n, k], f_r.at[n, k], src, g)
            when(full, src < nred, cp.wait_recv)

        each(1, C, f_wait)
        gq_ref[:, n * cw:(n + 1) * cw] = Fr[n].reshape(rows, cw)

    for k in range(1, Y):
        q_to_y(k).wait_send()
    q_to_sib.wait_send()
    for cp in fwd_copies:
        cp.wait_send()
    each(1, C, lambda k: l_copy(k).wait_send())
    for k in range(1, NQ):
        t_copy(k).wait_send()
    sh_copy.wait_send()
    for yy in range(Y):
        a_copy(yy).wait_send()
    for n in range(NC):
        for k in range(1, Y):
            b_copy(n, k).wait_send()

        def c_done(k, n=n):
            to, cp = c_copy(n, k)
            when(full, to < nred, cp.wait_send)

        each(1, C, c_done)
        when(full, c < nred, lambda n=n: each(1, C, lambda k: f_copy(n, k).wait_send()))
    for d in range(nd):
        pltpu.make_async_copy(gd.at[d], gd_hbm.at[d], gd_sem.at[d]).wait()


def per_device(C, NQ, queries, documents, candidates):
    nq, qlen, width = queries.shape
    nd, tok, _ = documents.shape
    rows = nq * qlen
    Y = NQ // 2
    rpc = max(16, rows // C)
    nred = rows // rpc
    NC = 2 if width % 256 == 0 else 1
    cw = width // NC
    dma = pltpu.SemaphoreType.DMA
    V = pltpu.VMEM
    loss, gq, gd = pl.pallas_call(
        functools.partial(kernel, C, NQ, qlen),
        out_shape=(
            jax.ShapeDtypeStruct((1, 1), f32),
            jax.ShapeDtypeStruct((rows, width), bf16),
            jax.ShapeDtypeStruct((nd, tok, width), bf16),
        ),
        in_specs=[
            pl.BlockSpec(memory_space=pltpu.SMEM),
            pl.BlockSpec(memory_space=pltpu.HBM),
            pl.BlockSpec(memory_space=pltpu.HBM),
        ],
        out_specs=(
            pl.BlockSpec(memory_space=pltpu.SMEM),
            pl.BlockSpec(memory_space=pltpu.VMEM),
            pl.BlockSpec(memory_space=pl.ANY),
        ),
        scratch_shapes=[
            V((NQ, rows, width), bf16),
            V((nd, tok, width), bf16),
            V((NQ, nd, tok, rows), f32),
            V((nd, NQ, rows, width), f32),
            V((nd * NQ, rows), f32),
            V((nd * NQ, rows), f32),
            V((C, nd * NQ, rows), f32),
            V((NQ, nd * NQ, rows), f32),
            V((nd * NQ, rows), f32),
            V((nd * NQ, rows), f32),
            V((nd * NQ, rows), f32),
            V((nd * NQ, rows), f32),
            V((Y, 2 * nd, rows, 128), f32),
            V((Y, nd, rows, width), bf16),
            V((Y, nd, rows, width), bf16),
            V((NC, Y, rows, cw), bf16),
            V((NC, Y, rows, cw), bf16),
            V((NC, rows, cw), f32),
            V((NC, nred, rpc, cw), bf16),
            V((NC, C, rpc, cw), bf16),
            V((NC, rpc, cw), bf16),
            V((NC, nred, rpc, cw), bf16),
            V((nd, tok, width), bf16),
            dma((nd,)), dma((nd,)), dma,
            dma((Y,)), dma((NQ,)), dma((Y,)),
            dma((C,)), dma((C,)),
            dma((NQ,)), dma((NQ,)), dma((2,)),
            dma((Y,)), dma((Y,)),
            dma((NC, Y)), dma((NC, Y)),
            dma((NC, C)), dma((NC, C)),
            dma((NC, C)), dma((NC, C)),
        ],
        compiler_params=pltpu.CompilerParams(
            collective_id=0, has_side_effects=True, vmem_limit_bytes=63 * 1024 * 1024),
    )(jnp.transpose(candidates), queries.reshape(rows, width), documents)
    return loss.reshape(()), gq.reshape(nq, qlen, width), gd


def solution(mesh):
    return jax.shard_map(
        functools.partial(per_device, mesh.shape["ctx"], mesh.shape["qg"]),
        mesh=mesh,
        in_specs=(P("qg", None, None), P("qg", "ctx", None), P()),
        out_specs=(P(), P("qg", None, None), P("qg", "ctx", None)),
        check_vma=False,
    )
```

```python
import functools

import jax
import jax.numpy as jnp
from jax import lax
from jax.experimental import pallas as pl
from jax.experimental.pallas import tpu as pltpu
from jax.sharding import PartitionSpec as P

sharpness_factor = 2.0
loss_scale = 1024.0
MESH = pl.DeviceIdType.MESH
f32 = jnp.float32
bf16 = jnp.bfloat16


def each(lo, hi, f):
    if hi - lo <= 16:
        for k in range(lo, hi):
            f(k)
    else:
        pl.loop(lo, hi)(f)


def when(always, cond, f):
    if always:
        f()
    else:
        pl.when(cond)(f)


def wrap(i, n):
    return lax.rem(i + 2 * n, n)


def kernel(
    C, NQ, qlen,
    cand_hbm, q_hbm, d_hbm,
    loss_ref, gq_ref, gd,
    Q, D, E, G, M, L, Lr, T, S, Sh, Shr, Ss, SC, As, Ar, Bs, Br, Mine, Cs, Cr, Fs, Fr, cand,
    d_sem, ql, cand_sem, qs, qr, fs, ls, lr, ts, tr, sh_sem, a_s, a_r, b_s, b_r, c_s, c_r, f_s, f_r,
):
    nd, tok, width = D.shape
    rows = Q.shape[1]
    Y = NQ // 2
    nq = rows // qlen
    slots = cand.shape[0]
    NC = Mine.shape[0]
    cw = width // NC
    rpc = Cr.shape[2]
    nred = rows // rpc
    full = nred == C
    c = lax.axis_index("ctx")
    g = lax.axis_index("qg")
    y = g // 2
    core = lax.rem(g, 2)
    sib = 2 * y + 1 - core

    def rc(src, dst, ssem, rsem, cc, gg):
        return pltpu.make_async_remote_copy(
            src_ref=src, dst_ref=dst, send_sem=ssem, recv_sem=rsem,
            device_id=(cc, gg), device_id_type=MESH,
        )

    barrier = pltpu.get_barrier_semaphore()
    for k in range(1, NQ):
        pl.semaphore_signal(barrier, inc=1, device_id=(c, wrap(g + k, NQ)), device_id_type=MESH)
    each(1, C, lambda k: pl.semaphore_signal(
        barrier, inc=1, device_id=(wrap(c + k, C), g), device_id_type=MESH))
    q_own = pltpu.make_async_copy(q_hbm, Q.at[g], ql)
    q_own.start()
    cand_copy = pltpu.make_async_copy(cand_hbm, cand, cand_sem)
    cand_copy.start()
    dcopy = [pltpu.make_async_copy(d_hbm.at[d], D.at[d], d_sem.at[d]) for d in range(nd)]
    for x in dcopy:
        x.start()
    pl.semaphore_wait(barrier, NQ - 1 + C - 1)

    def q_to_y(k):
        return rc(q_hbm, Q.at[g], qs.at[k], qr.at[g], c, wrap(g + 2 * k, NQ))

    q_to_sib = rc(q_hbm, Q.at[g], qs.at[0], qr.at[g], c, sib)
    for k in range(1, Y):
        q_to_y(k).start()
    q_to_sib.start()

    lane_q = lax.broadcasted_iota(jnp.int32, (NQ, rows), 1) // qlen
    sub_g = lax.broadcasted_iota(jnp.int32, (NQ, rows), 0)
    qid = sub_g * nq + lane_q
    ids = []
    cand_copy.wait()
    for k in range(slots):
        v = jnp.zeros((NQ, rows), jnp.int32)
        for q in range(cand.shape[1]):
            v = jnp.where(qid == q, cand[k, q], v)
        ids.append(v)

    def wait_q(src):
        rc(q_hbm, Q.at[src], qs.at[0], qr.at[src], c, sib).wait_recv()

    def fwd(first, n):
        qb = Q[pl.ds(first, n)].reshape(n * rows, width)
        for d in range(nd):
            lg = sharpness_factor * lax.dot_general(
                D[d], qb, (((1,), (1,)), ((), ())), preferred_element_type=f32)
            m = jnp.max(lg, axis=0, keepdims=True)
            e = jnp.exp(lg - m)
            lp = m + jnp.log(jnp.sum(e, axis=0, keepdims=True))
            for h in range(n):
                r = pl.ds(d * NQ + first + h, 1)
                E[first + h, d] = e[:, h * rows:(h + 1) * rows]
                M[r, :] = m[:, h * rows:(h + 1) * rows]
                L[r, :] = lp[:, h * rows:(h + 1) * rows]

    def a_copy(yb):
        return rc(As.at[yb], Ar.at[yb], a_s.at[yb], a_r.at[yb], c, sib)

    def gmat(yb):
        for d in range(nd):
            e = jnp.concatenate([E[2 * yb, d].astype(bf16), E[2 * yb + 1, d].astype(bf16)], axis=1)
            p = lax.dot_general(
                e, D[d], (((0,), (0,)), ((), ())), preferred_element_type=f32)
            G[d, pl.ds(2 * yb, 2)] = p.reshape(2, rows, width)
            As[yb, d] = G[d, 2 * yb + 1 - core].astype(bf16)
        a_copy(yb).start()

    q_own.wait()
    wait_q(sib)
    for x in dcopy:
        x.wait()
    fwd(2 * y, 2)
    gmat(y)
    fwd_copies = []
    for k in range(1, Y):
        src = wrap(g - 2 * k, NQ)
        wait_q(src)
        cp = rc(Q.at[src], Q.at[src], fs.at[k], qr.at[src], c, sib)
        cp.start()
        fwd_copies.append(cp)
        fwd(src, 1)
    for k in range(1, Y):
        src = wrap(sib - 2 * k, NQ)
        wait_q(src)
        fwd(src, 1)

    def l_copy(k):
        return rc(L, Lr.at[k], ls.at[k], lr.at[k], wrap(c + k, C), g)

    each(1, C, lambda k: l_copy(k).start())
    for k in range(1, Y):
        gmat(wrap(y - k, Y))
    Lr[0] = L[...]
    each(1, C, lambda k: l_copy(k).wait_recv())
    parts = Lr[...]
    top = jnp.max(parts, axis=0)
    lse = top + jnp.log(jnp.sum(jnp.exp(parts - top[None]), axis=0))

    lane = lax.broadcasted_iota(jnp.int32, lse.shape, 1)
    seg = lse
    step = 1
    while step < qlen:
        seg = seg + pltpu.roll(seg, step, 1)
        step *= 2
    seg = jnp.where(lax.rem(lane, qlen) == qlen - 1, seg, 0.0)
    step = 1
    while step < qlen:
        seg = seg + pltpu.roll(seg, rows - step, 1)
        step *= 2
    T[g] = seg / sharpness_factor

    def t_copy(k):
        return rc(T.at[g], T.at[g], ts.at[k], tr.at[k], c, wrap(g + k, NQ))

    for k in range(1, NQ):
        t_copy(k).start()
    Sh[...] = jnp.exp(M[...] - lse)
    sh_copy = rc(Sh, Shr, sh_sem.at[0], sh_sem.at[1], c, sib)
    sh_copy.start()
    for k in range(1, NQ):
        src = wrap(g - k, NQ)
        rc(T.at[src], T.at[src], ts.at[k], tr.at[k], c, src).wait_recv()

    pairs = []
    for k in range(slots):
        v = jnp.zeros((NQ, rows), f32)
        for gg in range(NQ):
            for d in range(nd):
                v = jnp.where(ids[k] == gg * nd + d, T[gg, d * NQ:(d + 1) * NQ, :], v)
        pairs.append(v)
    highest = functools.reduce(jnp.maximum, pairs)
    total = highest + jnp.log(functools.reduce(jnp.add, [jnp.exp(p - highest) for p in pairs]))
    loss_ref[0, 0] = jnp.sum(total - pairs[0]) / (NQ * rows)
    dz = [
        loss_scale / (NQ * nq) * (jnp.exp(p - total) - (1.0 if k == 0 else 0.0))
        for k, p in enumerate(pairs)
    ]
    sh_copy.wait_recv()
    for d in range(nd):
        r = slice(d * NQ, (d + 1) * NQ)
        for grp, shrink, dst in ((g, Sh, S), (sib, Shr, Ss)):
            w = jnp.zeros((NQ, rows), f32)
            for k in range(slots):
                w = w + jnp.where(ids[k] == grp * nd + d, dz[k], 0.0)
            dst[r, :] = w * shrink[r, :]
    own = [
        src[pl.ds(d * NQ + 2 * yy + core, 1), :]
        for yy in range(Y) for src in (S, Ss) for d in range(nd)
    ]
    St = jnp.transpose(jnp.concatenate(own, axis=0))
    for i in range(len(own)):
        SC[i // (2 * nd), i % (2 * nd)] = jnp.broadcast_to(St[:, i:i + 1], (rows, 128))

    for k in range(Y):
        a_copy(wrap(y - k, Y)).wait_recv()

    def scaled(yy, lo):
        at = slice(lo, lo + 128)
        v = SC[yy, 0] * G[0, 2 * yy + core, :, at]
        for d in range(1, nd):
            v = v + SC[yy, d] * G[d, 2 * yy + core, :, at]
        for d in range(nd):
            v = v + SC[yy, nd + d] * Ar[yy, d, :, at].astype(f32)
        return v

    def b_copy(n, k):
        return rc(Bs.at[n, k], Br.at[n, k], b_s.at[n, k], b_r.at[n, k], c, wrap(g + 2 * k, NQ))

    for n in range(NC):
        for k in range(1, Y):
            for lo in range(0, cw, 128):
                Bs[n, k, :, lo:lo + 128] = scaled(wrap(y + k, Y), n * cw + lo).astype(bf16)
            b_copy(n, k).start()
    for n in range(NC):
        for lo in range(0, cw, 128):
            Mine[n, :, lo:lo + 128] = scaled(y, n * cw + lo)

    for d in range(nd):
        acc = None
        for yb in range(Y):
            r = d * NQ + 2 * yb
            wt = jnp.concatenate(
                [(E[2 * yb + h, d] * S[r + h:r + h + 1, :]).astype(bf16) for h in range(2)], axis=1)
            part = jnp.dot(wt, Q[2 * yb:2 * yb + 2].reshape(2 * rows, width),
                           preferred_element_type=f32)
            acc = part if acc is None else acc + part
        gd[d] = acc.astype(bf16)

    share = lax.rem(c, nred)

    def c_copy(n, k):
        to = wrap(c + k, C)
        return to, rc(
            Cs.at[n, lax.rem(to, nred)], Cr.at[n, k], c_s.at[n, k], c_r.at[n, k], to, g)

    def f_copy(n, k):
        return rc(Fs.at[n], Fr.at[n, share], f_s.at[n, k], f_r.at[n, k], wrap(c + k, C), g)

    for n in range(NC):
        for k in range(1, Y):
            b_copy(n, k).wait_recv()
            Mine[n] = Mine[n] + Br[n, k].astype(f32)
        Cs[n] = Mine[n].astype(bf16).reshape(nred, rpc, cw)

        def c_start(k, n=n):
            to, cp = c_copy(n, k)
            when(full, to < nred, cp.start)

        each(1, C, c_start)

    for n in range(NC):
        def reduce_share(n=n):
            at = pl.multiple_of(share * rpc, rpc)
            Cr[n, 0] = jnp.zeros((rpc, cw), bf16)
            each(1, C, lambda k: c_copy(n, k)[1].wait_recv())
            v = Mine[n, pl.ds(at, rpc), :] + jnp.sum(Cr[n].astype(f32), axis=0)
            Fs[n] = v.astype(bf16)
            each(1, C, lambda k: f_copy(n, k).start())
            Fr[n, share] = Fs[n]

        when(full, c < nred, reduce_share)

    for n in range(NC):
        def f_wait(k, n=n):
            src = wrap(c - k, C)
            cp = rc(Fs.at[n], Fr.at[n, lax.rem(src, nred)], f_s.at[n, k], f_r.at[n, k], src, g)
            when(full, src < nred, cp.wait_recv)

        each(1, C, f_wait)
        gq_ref[:, n * cw:(n + 1) * cw] = Fr[n].reshape(rows, cw)

    for k in range(1, Y):
        q_to_y(k).wait_send()
    q_to_sib.wait_send()
    for cp in fwd_copies:
        cp.wait_send()
    each(1, C, lambda k: l_copy(k).wait_send())
    for k in range(1, NQ):
        t_copy(k).wait_send()
    sh_copy.wait_send()
    for yy in range(Y):
        a_copy(yy).wait_send()
    for n in range(NC):
        for k in range(1, Y):
            b_copy(n, k).wait_send()

        def c_done(k, n=n):
            to, cp = c_copy(n, k)
            when(full, to < nred, cp.wait_send)

        each(1, C, c_done)
        when(full, c < nred, lambda n=n: each(1, C, lambda k: f_copy(n, k).wait_send()))


def write_out(gq_in, gd_in, gq_out, gd_out, gq_sem, gd_sem):
    a = pltpu.make_async_copy(gd_in, gd_out, gd_sem)
    b = pltpu.make_async_copy(gq_in, gq_out, gq_sem)
    a.start()
    b.start()
    a.wait()
    b.wait()


def per_device(C, NQ, queries, documents, candidates):
    nq, qlen, width = queries.shape
    nd, tok, _ = documents.shape
    rows = nq * qlen
    Y = NQ // 2
    rpc = max(16, rows // C)
    nred = rows // rpc
    NC = 3 if width % 384 == 0 else 1
    cw = width // NC
    dma = pltpu.SemaphoreType.DMA
    V = pltpu.VMEM
    loss, gq, gd = pl.pallas_call(
        functools.partial(kernel, C, NQ, qlen),
        out_shape=(
            jax.ShapeDtypeStruct((1, 1), f32),
            pltpu.VMEM((rows, width), bf16),
            pltpu.VMEM((nd, tok, width), bf16),
        ),
        in_specs=[
            pl.BlockSpec(memory_space=pltpu.HBM),
            pl.BlockSpec(memory_space=pltpu.HBM),
            pl.BlockSpec(memory_space=pltpu.HBM),
        ],
        out_specs=(
            pl.BlockSpec(memory_space=pltpu.SMEM),
            pl.BlockSpec(memory_space=pltpu.VMEM),
            pl.BlockSpec(memory_space=pltpu.VMEM),
        ),
        scratch_shapes=[
            V((NQ, rows, width), bf16),
            V((nd, tok, width), bf16),
            V((NQ, nd, tok, rows), f32),
            V((nd, NQ, rows, width), f32),
            V((nd * NQ, rows), f32),
            V((nd * NQ, rows), f32),
            V((C, nd * NQ, rows), f32),
            V((NQ, nd * NQ, rows), f32),
            V((nd * NQ, rows), f32),
            V((nd * NQ, rows), f32),
            V((nd * NQ, rows), f32),
            V((nd * NQ, rows), f32),
            V((Y, 2 * nd, rows, 128), f32),
            V((Y, nd, rows, width), bf16),
            V((Y, nd, rows, width), bf16),
            V((NC, Y, rows, cw), bf16),
            V((NC, Y, rows, cw), bf16),
            V((NC, rows, cw), f32),
            V((NC, nred, rpc, cw), bf16),
            V((NC, C, rpc, cw), bf16),
            V((NC, rpc, cw), bf16),
            V((NC, nred, rpc, cw), bf16),
            pltpu.SMEM(candidates.shape[::-1], jnp.int32),
            dma((nd,)), dma, dma,
            dma((Y,)), dma((NQ,)), dma((Y,)),
            dma((C,)), dma((C,)),
            dma((NQ,)), dma((NQ,)), dma((2,)),
            dma((Y,)), dma((Y,)),
            dma((NC, Y)), dma((NC, Y)),
            dma((NC, C)), dma((NC, C)),
            dma((NC, C)), dma((NC, C)),
        ],
        compiler_params=pltpu.CompilerParams(
            collective_id=0, has_side_effects=True, vmem_limit_bytes=48 * 1024 * 1024),
    )(
        pltpu.with_memory_space_constraint(jnp.transpose(candidates), pltpu.HBM),
        pltpu.with_memory_space_constraint(queries.reshape(rows, width), pltpu.HBM),
        pltpu.with_memory_space_constraint(documents, pltpu.HBM),
    )
    gq, gd = pl.pallas_call(
        write_out,
        out_shape=(
            jax.ShapeDtypeStruct((rows, width), bf16),
            jax.ShapeDtypeStruct((nd, tok, width), bf16),
        ),
        in_specs=[pl.BlockSpec(memory_space=pl.ANY)] * 2,
        out_specs=(pl.BlockSpec(memory_space=pl.ANY),) * 2,
        scratch_shapes=[dma, dma],
    )(
        pltpu.with_memory_space_constraint(gq, pltpu.VMEM),
        pltpu.with_memory_space_constraint(gd, pltpu.VMEM),
    )
    return loss.reshape(()), gq.reshape(nq, qlen, width), gd


def solution(mesh):
    return jax.shard_map(
        functools.partial(per_device, mesh.shape["ctx"], mesh.shape["qg"]),
        mesh=mesh,
        in_specs=(P("qg", None, None), P("qg", "ctx", None), P()),
        out_specs=(P(), P("qg", None, None), P("qg", "ctx", None)),
        check_vma=False,
    )
```

```python
import functools

import jax
import jax.numpy as jnp
from jax import lax
from jax.experimental import pallas as pl
from jax.experimental.pallas import tpu as pltpu
from jax.sharding import PartitionSpec as P

sharpness_factor = 2.0
loss_scale = 1024.0
MESH = pl.DeviceIdType.MESH
f32 = jnp.float32
bf16 = jnp.bfloat16


def each(lo, hi, f):
    if hi - lo <= 16:
        for k in range(lo, hi):
            f(k)
    else:
        pl.loop(lo, hi)(f)


def when(always, cond, f):
    if always:
        f()
    else:
        pl.when(cond)(f)


def wrap(i, n):
    return lax.rem(i + 2 * n, n)


def kernel(
    C, NQ, qlen,
    cand_hbm, q_hbm, d_hbm,
    loss_ref, gq_ref, gd,
    Q, D, E, G, M, L, Lr, T, S, Sh, Shr, Ss, SC, As, Ar, Bs, Br, Mine, Xs, Xr, Half, Cs, Cr, Fs, Fr, cand,
    d_sem, ql, cand_sem, qs, qr, fs, ls, lr, ts, tr, sh_sem, a_s, a_r, b_s, b_r, x_s, x_r, c_s, c_r, f_s, f_r, h_s, h_r,
):
    nd, tok, width = D.shape
    rows = Q.shape[1]
    Y = NQ // 2
    nq = rows // qlen
    slots = cand.shape[0]
    NC = Mine.shape[0]
    cw = width // NC
    rpc = Cr.shape[2]
    half = rows // 2
    nred = half // rpc
    CZ = C // 2
    full = nred == CZ
    c = lax.axis_index("ctx")
    g = lax.axis_index("qg")
    m = c // 2
    b = lax.rem(c, 2)
    pair = 2 * m + 1 - b
    share = lax.rem(m, nred)
    y = g // 2
    core = lax.rem(g, 2)
    sib = 2 * y + 1 - core

    def rc(src, dst, ssem, rsem, cc, gg):
        return pltpu.make_async_remote_copy(
            src_ref=src, dst_ref=dst, send_sem=ssem, recv_sem=rsem,
            device_id=(cc, gg), device_id_type=MESH,
        )

    barrier = pltpu.get_barrier_semaphore()
    for k in range(1, NQ):
        pl.semaphore_signal(barrier, inc=1, device_id=(c, wrap(g + k, NQ)), device_id_type=MESH)
    each(1, C, lambda k: pl.semaphore_signal(
        barrier, inc=1, device_id=(wrap(c + k, C), g), device_id_type=MESH))
    q_own = pltpu.make_async_copy(q_hbm, Q.at[g], ql)
    q_own.start()
    cand_copy = pltpu.make_async_copy(cand_hbm, cand, cand_sem)
    cand_copy.start()
    dcopy = [pltpu.make_async_copy(d_hbm.at[d], D.at[d], d_sem.at[d]) for d in range(nd)]
    for x in dcopy:
        x.start()
    pl.semaphore_wait(barrier, NQ - 1 + C - 1)

    def q_to_y(k):
        return rc(q_hbm, Q.at[g], qs.at[k], qr.at[g], c, wrap(g + 2 * k, NQ))

    q_to_sib = rc(q_hbm, Q.at[g], qs.at[0], qr.at[g], c, sib)
    for k in range(1, Y):
        q_to_y(k).start()
    q_to_sib.start()

    lane_q = lax.broadcasted_iota(jnp.int32, (NQ, rows), 1) // qlen
    sub_g = lax.broadcasted_iota(jnp.int32, (NQ, rows), 0)
    qid = sub_g * nq + lane_q
    ids = []
    cand_copy.wait()
    for k in range(slots):
        v = jnp.zeros((NQ, rows), jnp.int32)
        for q in range(cand.shape[1]):
            v = jnp.where(qid == q, cand[k, q], v)
        ids.append(v)

    def wait_q(src):
        rc(q_hbm, Q.at[src], qs.at[0], qr.at[src], c, sib).wait_recv()

    def fwd(first, n):
        qb = Q[pl.ds(first, n)].reshape(n * rows, width)
        for d in range(nd):
            lg = sharpness_factor * lax.dot_general(
                D[d], qb, (((1,), (1,)), ((), ())), preferred_element_type=f32)
            mx = jnp.max(lg, axis=0, keepdims=True)
            e = jnp.exp(lg - mx)
            lp = mx + jnp.log(jnp.sum(e, axis=0, keepdims=True))
            for h in range(n):
                r = pl.ds(d * NQ + first + h, 1)
                E[first + h, d] = e[:, h * rows:(h + 1) * rows]
                M[r, :] = mx[:, h * rows:(h + 1) * rows]
                L[r, :] = lp[:, h * rows:(h + 1) * rows]

    def a_copy(yb):
        return rc(As.at[yb], Ar.at[yb], a_s.at[yb], a_r.at[yb], c, sib)

    def gmat(yb):
        for d in range(nd):
            e = jnp.concatenate([E[2 * yb, d].astype(bf16), E[2 * yb + 1, d].astype(bf16)], axis=1)
            p = lax.dot_general(
                e, D[d], (((0,), (0,)), ((), ())), preferred_element_type=f32)
            G[d, pl.ds(2 * yb, 2)] = p.reshape(2, rows, width)
            As[yb, d] = G[d, 2 * yb + 1 - core].astype(bf16)
        a_copy(yb).start()

    q_own.wait()
    wait_q(sib)
    for x in dcopy:
        x.wait()
    fwd(2 * y, 2)
    gmat(y)
    fwd_copies = []
    for k in range(1, Y):
        src = wrap(g - 2 * k, NQ)
        wait_q(src)
        cp = rc(Q.at[src], Q.at[src], fs.at[k], qr.at[src], c, sib)
        cp.start()
        fwd_copies.append(cp)
        fwd(src, 1)
    for k in range(1, Y):
        src = wrap(sib - 2 * k, NQ)
        wait_q(src)
        fwd(src, 1)

    def l_copy(k):
        return rc(L, Lr.at[k], ls.at[k], lr.at[k], wrap(c + k, C), g)

    each(1, C, lambda k: l_copy(k).start())
    for k in range(1, Y):
        gmat(wrap(y - k, Y))
    Lr[0] = L[...]
    each(1, C, lambda k: l_copy(k).wait_recv())
    parts = Lr[...]
    top = jnp.max(parts, axis=0)
    lse = top + jnp.log(jnp.sum(jnp.exp(parts - top[None]), axis=0))

    lane = lax.broadcasted_iota(jnp.int32, lse.shape, 1)
    seg = lse
    step = 1
    while step < qlen:
        seg = seg + pltpu.roll(seg, step, 1)
        step *= 2
    seg = jnp.where(lax.rem(lane, qlen) == qlen - 1, seg, 0.0)
    step = 1
    while step < qlen:
        seg = seg + pltpu.roll(seg, rows - step, 1)
        step *= 2
    T[g] = seg / sharpness_factor

    def t_copy(k):
        return rc(T.at[g], T.at[g], ts.at[k], tr.at[k], c, wrap(g + k, NQ))

    for k in range(1, NQ):
        t_copy(k).start()
    Sh[...] = jnp.exp(M[...] - lse)
    sh_copy = rc(Sh, Shr, sh_sem.at[0], sh_sem.at[1], c, sib)
    sh_copy.start()
    for k in range(1, NQ):
        src = wrap(g - k, NQ)
        rc(T.at[src], T.at[src], ts.at[k], tr.at[k], c, src).wait_recv()

    pairs = []
    for k in range(slots):
        v = jnp.zeros((NQ, rows), f32)
        for gg in range(NQ):
            for d in range(nd):
                v = jnp.where(ids[k] == gg * nd + d, T[gg, d * NQ:(d + 1) * NQ, :], v)
        pairs.append(v)
    highest = functools.reduce(jnp.maximum, pairs)
    total = highest + jnp.log(functools.reduce(jnp.add, [jnp.exp(p - highest) for p in pairs]))
    loss_ref[...] = jnp.sum(total - pairs[0]).reshape(1, 1) / (NQ * rows)
    dz = [
        loss_scale / (NQ * nq) * (jnp.exp(p - total) - (1.0 if k == 0 else 0.0))
        for k, p in enumerate(pairs)
    ]
    sh_copy.wait_recv()
    for d in range(nd):
        r = slice(d * NQ, (d + 1) * NQ)
        for grp, shrink, dst in ((g, Sh, S), (sib, Shr, Ss)):
            w = jnp.zeros((NQ, rows), f32)
            for k in range(slots):
                w = w + jnp.where(ids[k] == grp * nd + d, dz[k], 0.0)
            dst[r, :] = w * shrink[r, :]
    own = [
        src[pl.ds(d * NQ + 2 * yy + core, 1), :]
        for yy in range(Y) for src in (S, Ss) for d in range(nd)
    ]
    St = jnp.transpose(jnp.concatenate(own, axis=0))
    for i in range(len(own)):
        SC[i // (2 * nd), i % (2 * nd)] = jnp.broadcast_to(St[:, i:i + 1], (rows, 128))

    for k in range(Y):
        a_copy(wrap(y - k, Y)).wait_recv()

    def scaled(yy, lo):
        at = slice(lo, lo + 128)
        v = SC[yy, 0] * G[0, 2 * yy + core, :, at]
        for d in range(1, nd):
            v = v + SC[yy, d] * G[d, 2 * yy + core, :, at]
        for d in range(nd):
            v = v + SC[yy, nd + d] * Ar[yy, d, :, at].astype(f32)
        return v

    def b_copy(n, k):
        return rc(Bs.at[n, k], Br.at[n, k], b_s.at[n, k], b_r.at[n, k], c, wrap(g + 2 * k, NQ))

    for n in range(NC):
        for k in range(1, Y):
            for lo in range(0, cw, 128):
                Bs[n, k, :, lo:lo + 128] = scaled(wrap(y + k, Y), n * cw + lo).astype(bf16)
            b_copy(n, k).start()
    for n in range(NC):
        for lo in range(0, cw, 128):
            Mine[n, :, lo:lo + 128] = scaled(y, n * cw + lo)

    for d in range(nd):
        acc = None
        for yb in range(Y):
            r = d * NQ + 2 * yb
            wt = jnp.concatenate(
                [(E[2 * yb + h, d] * S[r + h:r + h + 1, :]).astype(bf16) for h in range(2)], axis=1)
            part = jnp.dot(wt, Q[2 * yb:2 * yb + 2].reshape(2 * rows, width),
                           preferred_element_type=f32)
            acc = part if acc is None else acc + part
        gd[d] = acc.astype(bf16)

    def x_copy(n):
        return rc(Xs.at[n], Xr.at[n], x_s.at[n], x_r.at[n], pair, g)

    def c_copy(n, k):
        to = wrap(m + k, CZ)
        return to, rc(
            Cs.at[n, lax.rem(to, nred)], Cr.at[n, k], c_s.at[n, k], c_r.at[n, k], 2 * to + b, g)

    def f_copy(n, k):
        return rc(Fs.at[n], Fr.at[n, b, share], f_s.at[n, k], f_r.at[n, k],
                  2 * wrap(m + k, CZ) + b, g)

    def h_copy(n):
        return rc(Fr.at[n, b], Fr.at[n, b], h_s.at[n], h_r.at[n], pair, g)

    keep = pl.ds(pl.multiple_of(b * half, half), half)
    give = pl.ds(pl.multiple_of((1 - b) * half, half), half)
    for n in range(NC):
        for k in range(1, Y):
            b_copy(n, k).wait_recv()
            Mine[n] = Mine[n] + Br[n, k].astype(f32)
        Xs[n] = Mine[n, give, :].astype(bf16)
        x_copy(n).start()

    for n in range(NC):
        x_copy(n).wait_recv()
        Half[n] = Mine[n, keep, :] + Xr[n].astype(f32)
        Cs[n] = Half[n].astype(bf16).reshape(nred, rpc, cw)

        def c_start(k, n=n):
            to, cp = c_copy(n, k)
            when(full, to < nred, cp.start)

        each(1, CZ, c_start)

    for n in range(NC):
        def reduce_share(n=n):
            at = pl.multiple_of(share * rpc, rpc)
            Cr[n, 0] = jnp.zeros((rpc, cw), bf16)
            each(1, CZ, lambda k: c_copy(n, k)[1].wait_recv())
            v = Half[n, pl.ds(at, rpc), :] + jnp.sum(Cr[n].astype(f32), axis=0)
            Fs[n] = v.astype(bf16)
            each(1, CZ, lambda k: f_copy(n, k).start())
            Fr[n, b, share] = Fs[n]

        when(full, m < nred, reduce_share)

    for n in range(NC):
        def f_wait(k, n=n):
            src = wrap(m - k, CZ)
            cp = rc(Fs.at[n], Fr.at[n, b, lax.rem(src, nred)], f_s.at[n, k], f_r.at[n, k],
                    2 * src + b, g)
            when(full, src < nred, cp.wait_recv)

        each(1, CZ, f_wait)
        h_copy(n).start()
    for n in range(NC):
        rc(Fr.at[n, 1 - b], Fr.at[n, 1 - b], h_s.at[n], h_r.at[n], pair, g).wait_recv()
        gq_ref[:, n * cw:(n + 1) * cw] = Fr[n].reshape(rows, cw)

    for k in range(1, Y):
        q_to_y(k).wait_send()
    q_to_sib.wait_send()
    for cp in fwd_copies:
        cp.wait_send()
    each(1, C, lambda k: l_copy(k).wait_send())
    for k in range(1, NQ):
        t_copy(k).wait_send()
    sh_copy.wait_send()
    for yy in range(Y):
        a_copy(yy).wait_send()
    for n in range(NC):
        for k in range(1, Y):
            b_copy(n, k).wait_send()

        x_copy(n).wait_send()
        h_copy(n).wait_send()

        def c_done(k, n=n):
            to, cp = c_copy(n, k)
            when(full, to < nred, cp.wait_send)

        each(1, CZ, c_done)
        when(full, m < nred, lambda n=n: each(1, CZ, lambda k: f_copy(n, k).wait_send()))


def write_out(*refs):
    n = len(refs) // 3
    copies = [pltpu.make_async_copy(refs[i], refs[n + i], refs[2 * n + i]) for i in range(n)]
    for x in copies:
        x.start()
    for x in copies:
        x.wait()


def per_device(C, NQ, queries, documents, candidates):
    nq, qlen, width = queries.shape
    nd, tok, _ = documents.shape
    rows = nq * qlen
    Y = NQ // 2
    half = rows // 2
    rpc = max(16, rows // C)
    nred = half // rpc
    CZ = C // 2
    NC = 3 if width % 384 == 0 else 1
    cw = width // NC
    dma = pltpu.SemaphoreType.DMA
    V = pltpu.VMEM
    loss, gq, gd = pl.pallas_call(
        functools.partial(kernel, C, NQ, qlen),
        out_shape=(
            pltpu.VMEM((1, 1), f32),
            pltpu.VMEM((rows, width), bf16),
            pltpu.VMEM((nd, tok, width), bf16),
        ),
        in_specs=[
            pl.BlockSpec(memory_space=pltpu.HBM),
            pl.BlockSpec(memory_space=pltpu.HBM),
            pl.BlockSpec(memory_space=pltpu.HBM),
        ],
        out_specs=(
            pl.BlockSpec(memory_space=pltpu.VMEM),
            pl.BlockSpec(memory_space=pltpu.VMEM),
            pl.BlockSpec(memory_space=pltpu.VMEM),
        ),
        scratch_shapes=[
            V((NQ, rows, width), bf16),
            V((nd, tok, width), bf16),
            V((NQ, nd, tok, rows), f32),
            V((nd, NQ, rows, width), f32),
            V((nd * NQ, rows), f32),
            V((nd * NQ, rows), f32),
            V((C, nd * NQ, rows), f32),
            V((NQ, nd * NQ, rows), f32),
            V((nd * NQ, rows), f32),
            V((nd * NQ, rows), f32),
            V((nd * NQ, rows), f32),
            V((nd * NQ, rows), f32),
            V((Y, 2 * nd, rows, 128), f32),
            V((Y, nd, rows, width), bf16),
            V((Y, nd, rows, width), bf16),
            V((NC, Y, rows, cw), bf16),
            V((NC, Y, rows, cw), bf16),
            V((NC, rows, cw), f32),
            V((NC, half, cw), bf16),
            V((NC, half, cw), bf16),
            V((NC, half, cw), f32),
            V((NC, nred, rpc, cw), bf16),
            V((NC, CZ, rpc, cw), bf16),
            V((NC, rpc, cw), bf16),
            V((NC, 2, nred, rpc, cw), bf16),
            pltpu.SMEM(candidates.shape[::-1], jnp.int32),
            dma((nd,)), dma, dma,
            dma((Y,)), dma((NQ,)), dma((Y,)),
            dma((C,)), dma((C,)),
            dma((NQ,)), dma((NQ,)), dma((2,)),
            dma((Y,)), dma((Y,)),
            dma((NC, Y)), dma((NC, Y)),
            dma((NC,)), dma((NC,)),
            dma((NC, CZ)), dma((NC, CZ)),
            dma((NC, CZ)), dma((NC, CZ)),
            dma((NC,)), dma((NC,)),
        ],
        compiler_params=pltpu.CompilerParams(
            collective_id=0, has_side_effects=True, vmem_limit_bytes=48 * 1024 * 1024),
    )(
        pltpu.with_memory_space_constraint(jnp.transpose(candidates), pltpu.HBM),
        pltpu.with_memory_space_constraint(queries.reshape(rows, width), pltpu.HBM),
        pltpu.with_memory_space_constraint(documents, pltpu.HBM),
    )
    loss, gq, gd = pl.pallas_call(
        write_out,
        out_shape=tuple(jax.ShapeDtypeStruct(x.shape, x.dtype) for x in (loss, gq, gd)),
        in_specs=[pl.BlockSpec(memory_space=pl.ANY)] * 3,
        out_specs=(pl.BlockSpec(memory_space=pl.ANY),) * 3,
        scratch_shapes=[dma] * 3,
    )(*(pltpu.with_memory_space_constraint(x, pltpu.VMEM) for x in (loss, gq, gd)))
    return loss.reshape(()), gq.reshape(nq, qlen, width), gd


def solution(mesh):
    return jax.shard_map(
        functools.partial(per_device, mesh.shape["ctx"], mesh.shape["qg"]),
        mesh=mesh,
        in_specs=(P("qg", None, None), P("qg", "ctx", None), P()),
        out_specs=(P(), P("qg", None, None), P("qg", "ctx", None)),
        check_vma=False,
    )
```

```python
import functools

import jax
import jax.numpy as jnp
from jax import lax
from jax.experimental import pallas as pl
from jax.experimental.pallas import tpu as pltpu
from jax.sharding import PartitionSpec as P

sharpness_factor = 2.0
loss_scale = 1024.0
MESH = pl.DeviceIdType.MESH
f32 = jnp.float32
bf16 = jnp.bfloat16


def each(lo, hi, f):
    if hi - lo <= 16:
        for k in range(lo, hi):
            f(k)
    else:
        pl.loop(lo, hi)(f)


def when(always, cond, f):
    if always:
        f()
    else:
        pl.when(cond)(f)


def wrap(i, n):
    return lax.rem(i + 2 * n, n)


def kernel(
    C, NQ, qlen,
    cand_hbm, q_hbm, d_hbm,
    loss_ref, gq_ref, gd,
    Q, D, E, G, M, L, Lr, T, S, Sh, Shr, Ss, SC, As, Ar, Bs, Br, Mine, Cs, Cr, Fs, Fr, cand,
    d_sem, ql, cand_sem, qs, qr, fs, ls, lr, ts, tr, sh_sem, a_s, a_r, b_s, b_r, c_s, c_r, f_s, f_r,
):
    nd, tok, width = D.shape
    rows = Q.shape[1]
    Y = NQ // 2
    nq = rows // qlen
    slots = cand.shape[0]
    NC = Mine.shape[0]
    cw = width // NC
    rpc = Cr.shape[2]
    nred = rows // rpc
    full = nred == C
    c = lax.axis_index("ctx")
    g = lax.axis_index("qg")
    y = g // 2
    core = lax.rem(g, 2)
    sib = 2 * y + 1 - core

    def rc(src, dst, ssem, rsem, cc, gg):
        return pltpu.make_async_remote_copy(
            src_ref=src, dst_ref=dst, send_sem=ssem, recv_sem=rsem,
            device_id=(cc, gg), device_id_type=MESH,
        )

    barrier = pltpu.get_barrier_semaphore()
    for k in range(1, NQ):
        pl.semaphore_signal(barrier, inc=1, device_id=(c, wrap(g + k, NQ)), device_id_type=MESH)
    each(1, C, lambda k: pl.semaphore_signal(
        barrier, inc=1, device_id=(wrap(c + k, C), g), device_id_type=MESH))
    q_own = pltpu.make_async_copy(q_hbm, Q.at[g], ql)
    q_own.start()
    cand_copy = pltpu.make_async_copy(cand_hbm, cand, cand_sem)
    cand_copy.start()
    dcopy = [pltpu.make_async_copy(d_hbm.at[d], D.at[d], d_sem.at[d]) for d in range(nd)]
    for x in dcopy:
        x.start()
    pl.semaphore_wait(barrier, NQ - 1 + C - 1)

    def q_to_y(k):
        return rc(q_hbm, Q.at[g], qs.at[k], qr.at[g], c, wrap(g + 2 * k, NQ))

    q_to_sib = rc(q_hbm, Q.at[g], qs.at[0], qr.at[g], c, sib)
    for k in range(1, Y):
        q_to_y(k).start()
    q_to_sib.start()

    lane_q = lax.broadcasted_iota(jnp.int32, (NQ, rows), 1) // qlen
    sub_g = lax.broadcasted_iota(jnp.int32, (NQ, rows), 0)
    qid = sub_g * nq + lane_q
    ids = []
    cand_copy.wait()
    for k in range(slots):
        v = jnp.zeros((NQ, rows), jnp.int32)
        for q in range(cand.shape[1]):
            v = jnp.where(qid == q, cand[k, q], v)
        ids.append(v)

    def wait_q(src):
        rc(q_hbm, Q.at[src], qs.at[0], qr.at[src], c, sib).wait_recv()

    def fwd(first, n):
        qb = Q[pl.ds(first, n)].reshape(n * rows, width)
        for d in range(nd):
            lg = sharpness_factor * lax.dot_general(
                D[d], qb, (((1,), (1,)), ((), ())), preferred_element_type=f32)
            m = jnp.max(lg, axis=0, keepdims=True)
            e = jnp.exp(lg - m)
            lp = m + jnp.log(jnp.sum(e, axis=0, keepdims=True))
            for h in range(n):
                r = pl.ds(d * NQ + first + h, 1)
                E[first + h, d] = e[:, h * rows:(h + 1) * rows]
                M[r, :] = m[:, h * rows:(h + 1) * rows]
                L[r, :] = lp[:, h * rows:(h + 1) * rows]

    def a_copy(yb):
        return rc(As.at[yb], Ar.at[yb], a_s.at[yb], a_r.at[yb], c, sib)

    def gmat(yb):
        for d in range(nd):
            e = jnp.concatenate([E[2 * yb, d].astype(bf16), E[2 * yb + 1, d].astype(bf16)], axis=1)
            p = lax.dot_general(
                e, D[d], (((0,), (0,)), ((), ())), preferred_element_type=f32)
            G[d, pl.ds(2 * yb, 2)] = p.reshape(2, rows, width)
            As[yb, d] = G[d, 2 * yb + 1 - core].astype(bf16)
        a_copy(yb).start()

    q_own.wait()
    wait_q(sib)
    for x in dcopy:
        x.wait()
    fwd(2 * y, 2)
    gmat(y)
    fwd_copies = []
    for k in range(1, Y):
        src = wrap(g - 2 * k, NQ)
        wait_q(src)
        cp = rc(Q.at[src], Q.at[src], fs.at[k], qr.at[src], c, sib)
        cp.start()
        fwd_copies.append(cp)
        fwd(src, 1)
    for k in range(1, Y):
        src = wrap(sib - 2 * k, NQ)
        wait_q(src)
        fwd(src, 1)

    def l_copy(k):
        return rc(L, Lr.at[k], ls.at[k], lr.at[k], wrap(c + k, C), g)

    each(1, C, lambda k: l_copy(k).start())
    for k in range(1, Y):
        gmat(wrap(y - k, Y))
    Lr[0] = L[...]
    each(1, C, lambda k: l_copy(k).wait_recv())
    parts = Lr[...]
    top = jnp.max(parts, axis=0)
    lse = top + jnp.log(jnp.sum(jnp.exp(parts - top[None]), axis=0))

    same = (lax.broadcasted_iota(jnp.int32, (rows, rows), 0) // qlen
            == lax.broadcasted_iota(jnp.int32, (rows, rows), 1) // qlen).astype(f32)
    T[g] = lax.dot_general(
        lse, same, (((1,), (0,)), ((), ())),
        precision=lax.Precision.HIGHEST, preferred_element_type=f32) / sharpness_factor

    def t_copy(k):
        return rc(T.at[g], T.at[g], ts.at[k], tr.at[k], c, wrap(g + k, NQ))

    for k in range(1, NQ):
        t_copy(k).start()
    Sh[...] = jnp.exp(M[...] - lse)
    sh_copy = rc(Sh, Shr, sh_sem.at[0], sh_sem.at[1], c, sib)
    sh_copy.start()
    for k in range(1, NQ):
        src = wrap(g - k, NQ)
        rc(T.at[src], T.at[src], ts.at[k], tr.at[k], c, src).wait_recv()

    pairs = []
    for k in range(slots):
        v = jnp.zeros((NQ, rows), f32)
        for gg in range(NQ):
            for d in range(nd):
                v = jnp.where(ids[k] == gg * nd + d, T[gg, d * NQ:(d + 1) * NQ, :], v)
        pairs.append(v)
    highest = functools.reduce(jnp.maximum, pairs)
    total = highest + jnp.log(functools.reduce(jnp.add, [jnp.exp(p - highest) for p in pairs]))
    loss_ref[0, 0] = jnp.sum(total - pairs[0]) / (NQ * rows)
    dz = [
        loss_scale / (NQ * nq) * (jnp.exp(p - total) - (1.0 if k == 0 else 0.0))
        for k, p in enumerate(pairs)
    ]
    sh_copy.wait_recv()
    for d in range(nd):
        r = slice(d * NQ, (d + 1) * NQ)
        for grp, shrink, dst in ((g, Sh, S), (sib, Shr, Ss)):
            w = jnp.zeros((NQ, rows), f32)
            for k in range(slots):
                w = w + jnp.where(ids[k] == grp * nd + d, dz[k], 0.0)
            dst[r, :] = w * shrink[r, :]
    own = [
        src[pl.ds(d * NQ + 2 * yy + core, 1), :]
        for yy in range(Y) for src in (S, Ss) for d in range(nd)
    ]
    St = jnp.transpose(jnp.concatenate(own, axis=0))
    for i in range(len(own)):
        SC[i // (2 * nd), i % (2 * nd)] = jnp.broadcast_to(St[:, i:i + 1], (rows, 128))

    for k in range(Y):
        a_copy(wrap(y - k, Y)).wait_recv()

    def scaled(yy, lo):
        at = slice(lo, lo + 128)
        v = SC[yy, 0] * G[0, 2 * yy + core, :, at]
        for d in range(1, nd):
            v = v + SC[yy, d] * G[d, 2 * yy + core, :, at]
        for d in range(nd):
            v = v + SC[yy, nd + d] * Ar[yy, d, :, at].astype(f32)
        return v

    def b_copy(n, k):
        return rc(Bs.at[n, k], Br.at[n, k], b_s.at[n, k], b_r.at[n, k], c, wrap(g + 2 * k, NQ))

    for n in range(NC):
        for k in range(1, Y):
            for lo in range(0, cw, 128):
                Bs[n, k, :, lo:lo + 128] = scaled(wrap(y + k, Y), n * cw + lo).astype(bf16)
            b_copy(n, k).start()
    for n in range(NC):
        for lo in range(0, cw, 128):
            Mine[n, :, lo:lo + 128] = scaled(y, n * cw + lo)

    def doc_grad(d):
        acc = None
        for yb in range(Y):
            r = d * NQ + 2 * yb
            wt = jnp.concatenate(
                [(E[2 * yb + h, d] * S[r + h:r + h + 1, :]).astype(bf16) for h in range(2)], axis=1)
            part = jnp.dot(wt, Q[2 * yb:2 * yb + 2].reshape(2 * rows, width),
                           preferred_element_type=f32)
            acc = part if acc is None else acc + part
        gd[d] = acc.astype(bf16)

    for d in range(nd // 2):
        doc_grad(d)

    share = lax.rem(c, nred)

    def c_copy(n, k):
        to = wrap(c + k, C)
        return to, rc(
            Cs.at[n, lax.rem(to, nred)], Cr.at[n, k], c_s.at[n, k], c_r.at[n, k], to, g)

    def f_copy(n, k):
        return rc(Fs.at[n], Fr.at[n, share], f_s.at[n, k], f_r.at[n, k], wrap(c + k, C), g)

    for n in range(NC):
        for k in range(1, Y):
            b_copy(n, k).wait_recv()
            Mine[n] = Mine[n] + Br[n, k].astype(f32)
        Cs[n] = Mine[n].astype(bf16).reshape(nred, rpc, cw)

        def c_start(k, n=n):
            to, cp = c_copy(n, k)
            when(full, to < nred, cp.start)

        each(1, C, c_start)

    for d in range(nd // 2, nd):
        doc_grad(d)

    for n in range(NC):
        def reduce_share(n=n):
            at = pl.multiple_of(share * rpc, rpc)
            Cr[n, 0] = jnp.zeros((rpc, cw), bf16)
            each(1, C, lambda k: c_copy(n, k)[1].wait_recv())
            v = Mine[n, pl.ds(at, rpc), :] + jnp.sum(Cr[n].astype(f32), axis=0)
            Fs[n] = v.astype(bf16)
            each(1, C, lambda k: f_copy(n, k).start())
            Fr[n, share] = Fs[n]

        when(full, c < nred, reduce_share)

    for n in range(NC):
        def f_wait(k, n=n):
            src = wrap(c - k, C)
            cp = rc(Fs.at[n], Fr.at[n, lax.rem(src, nred)], f_s.at[n, k], f_r.at[n, k], src, g)
            when(full, src < nred, cp.wait_recv)

        each(1, C, f_wait)
        gq_ref[:, n * cw:(n + 1) * cw] = Fr[n].reshape(rows, cw)

    for k in range(1, Y):
        q_to_y(k).wait_send()
    q_to_sib.wait_send()
    for cp in fwd_copies:
        cp.wait_send()
    each(1, C, lambda k: l_copy(k).wait_send())
    for k in range(1, NQ):
        t_copy(k).wait_send()
    sh_copy.wait_send()
    for yy in range(Y):
        a_copy(yy).wait_send()
    for n in range(NC):
        for k in range(1, Y):
            b_copy(n, k).wait_send()

        def c_done(k, n=n):
            to, cp = c_copy(n, k)
            when(full, to < nred, cp.wait_send)

        each(1, C, c_done)
        when(full, c < nred, lambda n=n: each(1, C, lambda k: f_copy(n, k).wait_send()))


def write_out(gq_in, gd_in, gq_out, gd_out, gq_sem, gd_sem):
    a = pltpu.make_async_copy(gd_in, gd_out, gd_sem)
    b = pltpu.make_async_copy(gq_in, gq_out, gq_sem)
    a.start()
    b.start()
    a.wait()
    b.wait()


def per_device(C, NQ, queries, documents, candidates):
    nq, qlen, width = queries.shape
    nd, tok, _ = documents.shape
    rows = nq * qlen
    Y = NQ // 2
    rpc = max(16, rows // C)
    nred = rows // rpc
    NC = 3 if width % 384 == 0 else 1
    cw = width // NC
    dma = pltpu.SemaphoreType.DMA
    V = pltpu.VMEM
    loss, gq, gd = pl.pallas_call(
        functools.partial(kernel, C, NQ, qlen),
        out_shape=(
            jax.ShapeDtypeStruct((1, 1), f32),
            pltpu.VMEM((rows, width), bf16),
            pltpu.VMEM((nd, tok, width), bf16),
        ),
        in_specs=[
            pl.BlockSpec(memory_space=pltpu.HBM),
            pl.BlockSpec(memory_space=pltpu.HBM),
            pl.BlockSpec(memory_space=pltpu.HBM),
        ],
        out_specs=(
            pl.BlockSpec(memory_space=pltpu.SMEM),
            pl.BlockSpec(memory_space=pltpu.VMEM),
            pl.BlockSpec(memory_space=pltpu.VMEM),
        ),
        scratch_shapes=[
            V((NQ, rows, width), bf16),
            V((nd, tok, width), bf16),
            V((NQ, nd, tok, rows), f32),
            V((nd, NQ, rows, width), f32),
            V((nd * NQ, rows), f32),
            V((nd * NQ, rows), f32),
            V((C, nd * NQ, rows), f32),
            V((NQ, nd * NQ, rows), f32),
            V((nd * NQ, rows), f32),
            V((nd * NQ, rows), f32),
            V((nd * NQ, rows), f32),
            V((nd * NQ, rows), f32),
            V((Y, 2 * nd, rows, 128), f32),
            V((Y, nd, rows, width), bf16),
            V((Y, nd, rows, width), bf16),
            V((NC, Y, rows, cw), bf16),
            V((NC, Y, rows, cw), bf16),
            V((NC, rows, cw), f32),
            V((NC, nred, rpc, cw), bf16),
            V((NC, C, rpc, cw), bf16),
            V((NC, rpc, cw), bf16),
            V((NC, nred, rpc, cw), bf16),
            pltpu.SMEM(candidates.shape[::-1], jnp.int32),
            dma((nd,)), dma, dma,
            dma((Y,)), dma((NQ,)), dma((Y,)),
            dma((C,)), dma((C,)),
            dma((NQ,)), dma((NQ,)), dma((2,)),
            dma((Y,)), dma((Y,)),
            dma((NC, Y)), dma((NC, Y)),
            dma((NC, C)), dma((NC, C)),
            dma((NC, C)), dma((NC, C)),
        ],
        compiler_params=pltpu.CompilerParams(
            collective_id=0, has_side_effects=True, vmem_limit_bytes=48 * 1024 * 1024),
    )(
        pltpu.with_memory_space_constraint(jnp.transpose(candidates), pltpu.HBM),
        pltpu.with_memory_space_constraint(queries.reshape(rows, width), pltpu.HBM),
        pltpu.with_memory_space_constraint(documents, pltpu.HBM),
    )
    gq, gd = pl.pallas_call(
        write_out,
        out_shape=(
            jax.ShapeDtypeStruct((rows, width), bf16),
            jax.ShapeDtypeStruct((nd, tok, width), bf16),
        ),
        in_specs=[pl.BlockSpec(memory_space=pl.ANY)] * 2,
        out_specs=(pl.BlockSpec(memory_space=pl.ANY),) * 2,
        scratch_shapes=[dma, dma],
    )(
        pltpu.with_memory_space_constraint(gq, pltpu.VMEM),
        pltpu.with_memory_space_constraint(gd, pltpu.VMEM),
    )
    return loss.reshape(()), gq.reshape(nq, qlen, width), gd


def solution(mesh):
    return jax.shard_map(
        functools.partial(per_device, mesh.shape["ctx"], mesh.shape["qg"]),
        mesh=mesh,
        in_specs=(P("qg", None, None), P("qg", "ctx", None), P()),
        out_specs=(P(), P("qg", None, None), P("qg", "ctx", None)),
        check_vma=False,
    )
```

```python
import functools

import jax
import jax.numpy as jnp
from jax import lax
from jax.experimental import pallas as pl
from jax.experimental.pallas import tpu as pltpu
from jax.sharding import PartitionSpec as P

sharpness_factor = 2.0
loss_scale = 1024.0
MESH = pl.DeviceIdType.MESH
f32 = jnp.float32
bf16 = jnp.bfloat16


def each(lo, hi, f):
    if hi - lo <= 16:
        for k in range(lo, hi):
            f(k)
    else:
        pl.loop(lo, hi)(f)


def when(always, cond, f):
    if always:
        f()
    else:
        pl.when(cond)(f)


def wrap(i, n):
    return lax.rem(i + 2 * n, n)


def kernel(
    C, NQ, qlen,
    cand_hbm, q_hbm, d_hbm,
    loss_ref, gq_ref, gd,
    Q, D, E, G, M, L, Lr, T, S, Sh, Shr, Ss, SC, As, Ar, Bs, Br, Mine, Cs, Cr, Fs, Fr, cand,
    d_sem, ql, cand_sem, qs, qr, fs, ls, lr, ts, tr, sh_sem, a_s, a_r, b_s, b_r, c_s, c_r, f_s, f_r,
):
    nd, tok, width = D.shape
    rows = Q.shape[1]
    Y = NQ // 2
    nq = rows // qlen
    slots = cand.shape[0]
    NC = Mine.shape[0]
    cw = width // NC
    rpc = Cr.shape[2]
    half = rows // 2
    nred = half // rpc
    CZ = C // 2
    full = nred == CZ
    c = lax.axis_index("ctx")
    g = lax.axis_index("qg")
    m = c // 2
    b = lax.rem(c, 2)
    y = g // 2
    core = lax.rem(g, 2)
    sib = 2 * y + 1 - core

    def rc(src, dst, ssem, rsem, cc, gg):
        return pltpu.make_async_remote_copy(
            src_ref=src, dst_ref=dst, send_sem=ssem, recv_sem=rsem,
            device_id=(cc, gg), device_id_type=MESH,
        )

    barrier = pltpu.get_barrier_semaphore()
    for k in range(1, NQ):
        pl.semaphore_signal(barrier, inc=1, device_id=(c, wrap(g + k, NQ)), device_id_type=MESH)
    each(1, C, lambda k: pl.semaphore_signal(
        barrier, inc=1, device_id=(wrap(c + k, C), g), device_id_type=MESH))
    for k in range(1, Y):
        pl.semaphore_signal(
            barrier, inc=1, device_id=(2 * m + 1 - b, wrap(g + 2 * k, NQ)), device_id_type=MESH)
    q_own = pltpu.make_async_copy(q_hbm, Q.at[g], ql)
    q_own.start()
    cand_copy = pltpu.make_async_copy(cand_hbm, cand, cand_sem)
    cand_copy.start()
    dcopy = [pltpu.make_async_copy(d_hbm.at[d], D.at[d], d_sem.at[d]) for d in range(nd)]
    for x in dcopy:
        x.start()
    pl.semaphore_wait(barrier, NQ - 1 + C - 1 + Y - 1)

    def q_to_y(k):
        return rc(q_hbm, Q.at[g], qs.at[k], qr.at[g], c, wrap(g + 2 * k, NQ))

    q_to_sib = rc(q_hbm, Q.at[g], qs.at[0], qr.at[g], c, sib)
    for k in range(1, Y):
        q_to_y(k).start()
    q_to_sib.start()

    lane_q = lax.broadcasted_iota(jnp.int32, (NQ, rows), 1) // qlen
    sub_g = lax.broadcasted_iota(jnp.int32, (NQ, rows), 0)
    qid = sub_g * nq + lane_q
    ids = []
    cand_copy.wait()
    for k in range(slots):
        v = jnp.zeros((NQ, rows), jnp.int32)
        for q in range(cand.shape[1]):
            v = jnp.where(qid == q, cand[k, q], v)
        ids.append(v)

    def wait_q(src):
        rc(q_hbm, Q.at[src], qs.at[0], qr.at[src], c, sib).wait_recv()

    def fwd(first, n):
        qb = Q[pl.ds(first, n)].reshape(n * rows, width)
        for d in range(nd):
            lg = sharpness_factor * lax.dot_general(
                D[d], qb, (((1,), (1,)), ((), ())), preferred_element_type=f32)
            m = jnp.max(lg, axis=0, keepdims=True)
            e = jnp.exp(lg - m)
            lp = m + jnp.log(jnp.sum(e, axis=0, keepdims=True))
            for h in range(n):
                r = pl.ds(d * NQ + first + h, 1)
                E[first + h, d] = e[:, h * rows:(h + 1) * rows]
                M[r, :] = m[:, h * rows:(h + 1) * rows]
                L[r, :] = lp[:, h * rows:(h + 1) * rows]

    def a_copy(yb):
        return rc(As.at[yb], Ar.at[yb], a_s.at[yb], a_r.at[yb], c, sib)

    def gmat(yb):
        for d in range(nd):
            e = jnp.concatenate([E[2 * yb, d].astype(bf16), E[2 * yb + 1, d].astype(bf16)], axis=1)
            p = lax.dot_general(
                e, D[d], (((0,), (0,)), ((), ())), preferred_element_type=f32)
            G[d, pl.ds(2 * yb, 2)] = p.reshape(2, rows, width)
            As[yb, d] = G[d, 2 * yb + 1 - core].astype(bf16)
        a_copy(yb).start()

    q_own.wait()
    wait_q(sib)
    for x in dcopy:
        x.wait()
    fwd(2 * y, 2)
    gmat(y)
    fwd_copies = []
    for k in range(1, Y):
        src = wrap(g - 2 * k, NQ)
        wait_q(src)
        cp = rc(Q.at[src], Q.at[src], fs.at[k], qr.at[src], c, sib)
        cp.start()
        fwd_copies.append(cp)
        fwd(src, 1)
    for k in range(1, Y):
        src = wrap(sib - 2 * k, NQ)
        wait_q(src)
        fwd(src, 1)

    def l_copy(k):
        return rc(L, Lr.at[k], ls.at[k], lr.at[k], wrap(c + k, C), g)

    each(1, C, lambda k: l_copy(k).start())
    for k in range(1, Y):
        gmat(wrap(y - k, Y))
    Lr[0] = L[...]
    each(1, C, lambda k: l_copy(k).wait_recv())
    parts = Lr[...]
    top = jnp.max(parts, axis=0)
    lse = top + jnp.log(jnp.sum(jnp.exp(parts - top[None]), axis=0))

    same = (lax.broadcasted_iota(jnp.int32, (rows, rows), 0) // qlen
            == lax.broadcasted_iota(jnp.int32, (rows, rows), 1) // qlen).astype(f32)
    T[g] = lax.dot_general(
        lse, same, (((1,), (0,)), ((), ())),
        precision=lax.Precision.HIGHEST, preferred_element_type=f32) / sharpness_factor

    def t_copy(k):
        return rc(T.at[g], T.at[g], ts.at[k], tr.at[k], c, wrap(g + k, NQ))

    for k in range(1, NQ):
        t_copy(k).start()
    Sh[...] = jnp.exp(M[...] - lse)
    sh_copy = rc(Sh, Shr, sh_sem.at[0], sh_sem.at[1], c, sib)
    sh_copy.start()
    for k in range(1, NQ):
        src = wrap(g - k, NQ)
        rc(T.at[src], T.at[src], ts.at[k], tr.at[k], c, src).wait_recv()

    pairs = []
    for k in range(slots):
        v = jnp.zeros((NQ, rows), f32)
        for gg in range(NQ):
            for d in range(nd):
                v = jnp.where(ids[k] == gg * nd + d, T[gg, d * NQ:(d + 1) * NQ, :], v)
        pairs.append(v)
    highest = functools.reduce(jnp.maximum, pairs)
    total = highest + jnp.log(functools.reduce(jnp.add, [jnp.exp(p - highest) for p in pairs]))
    loss_ref[0, 0] = jnp.sum(total - pairs[0]) / (NQ * rows)
    dz = [
        loss_scale / (NQ * nq) * (jnp.exp(p - total) - (1.0 if k == 0 else 0.0))
        for k, p in enumerate(pairs)
    ]
    sh_copy.wait_recv()
    for d in range(nd):
        r = slice(d * NQ, (d + 1) * NQ)
        for grp, shrink, dst in ((g, Sh, S), (sib, Shr, Ss)):
            w = jnp.zeros((NQ, rows), f32)
            for k in range(slots):
                w = w + jnp.where(ids[k] == grp * nd + d, dz[k], 0.0)
            dst[r, :] = w * shrink[r, :]
    own = [
        src[pl.ds(d * NQ + 2 * yy + core, 1), :]
        for yy in range(Y) for src in (S, Ss) for d in range(nd)
    ]
    St = jnp.transpose(jnp.concatenate(own, axis=0))
    for i in range(len(own)):
        SC[i // (2 * nd), i % (2 * nd)] = jnp.broadcast_to(St[:, i:i + 1], (rows, 128))

    for k in range(Y):
        a_copy(wrap(y - k, Y)).wait_recv()

    def scaled(yy, h, lo):
        at = slice(lo, lo + 128)
        r = pl.ds(pl.multiple_of(h * half, half), half)
        v = SC[yy, 0, r, :] * G[0, 2 * yy + core, r, at]
        for d in range(1, nd):
            v = v + SC[yy, d, r, :] * G[d, 2 * yy + core, r, at]
        for d in range(nd):
            v = v + SC[yy, nd + d, r, :] * Ar[yy, d, r, at].astype(f32)
        return v

    u = 2 * y + b

    def b_copy(n, k):
        to = wrap(u + k, 2 * Y)
        return to, rc(Bs.at[n, k], Br.at[n, k], b_s.at[n, k], b_r.at[n, k],
                      2 * m + lax.rem(to, 2), 2 * (to // 2) + core)

    for n in range(NC):
        for k in range(1, 2 * Y):
            to, cp = b_copy(n, k)
            for lo in range(0, cw, 128):
                Bs[n, k, :, lo:lo + 128] = scaled(
                    to // 2, lax.rem(to, 2), n * cw + lo).astype(bf16)
            cp.start()
    for n in range(NC):
        for lo in range(0, cw, 128):
            Mine[n, :, lo:lo + 128] = scaled(y, b, n * cw + lo)

    def doc_grad(d):
        acc = None
        for yb in range(Y):
            r = d * NQ + 2 * yb
            wt = jnp.concatenate(
                [(E[2 * yb + h, d] * S[r + h:r + h + 1, :]).astype(bf16) for h in range(2)], axis=1)
            part = jnp.dot(wt, Q[2 * yb:2 * yb + 2].reshape(2 * rows, width),
                           preferred_element_type=f32)
            acc = part if acc is None else acc + part
        gd[d] = acc.astype(bf16)

    for d in range(nd // 2):
        doc_grad(d)

    share = lax.rem(m, nred)

    def c_copy(n, k):
        to = wrap(m + k, CZ)
        return to, rc(
            Cs.at[n, lax.rem(to, nred)], Cr.at[n, k], c_s.at[n, k], c_r.at[n, k], 2 * to + b, g)

    def f_copy(n, k):
        return rc(Fs.at[n], Fr.at[n, b, share], f_s.at[n, k], f_r.at[n, k], wrap(c + k, C), g)

    for n in range(NC):
        for k in range(1, 2 * Y):
            b_copy(n, k)[1].wait_recv()
            Mine[n] = Mine[n] + Br[n, k].astype(f32)
        Cs[n] = Mine[n].astype(bf16).reshape(nred, rpc, cw)

        def c_start(k, n=n):
            to, cp = c_copy(n, k)
            when(full, to < nred, cp.start)

        each(1, CZ, c_start)

    for d in range(nd // 2, nd):
        doc_grad(d)

    for n in range(NC):
        def reduce_share(n=n):
            at = pl.multiple_of(share * rpc, rpc)
            Cr[n, 0] = jnp.zeros((rpc, cw), bf16)
            each(1, CZ, lambda k: c_copy(n, k)[1].wait_recv())
            v = Mine[n, pl.ds(at, rpc), :] + jnp.sum(Cr[n].astype(f32), axis=0)
            Fs[n] = v.astype(bf16)
            each(1, C, lambda k: f_copy(n, k).start())
            Fr[n, b, share] = Fs[n]

        when(full, m < nred, reduce_share)

    for n in range(NC):
        def f_wait(k, n=n):
            src = wrap(c - k, C)
            cp = rc(Fs.at[n], Fr.at[n, lax.rem(src, 2), lax.rem(src // 2, nred)],
                    f_s.at[n, k], f_r.at[n, k], src, g)
            when(full, src // 2 < nred, cp.wait_recv)

        each(1, C, f_wait)
        gq_ref[:, n * cw:(n + 1) * cw] = Fr[n].reshape(rows, cw)

    for k in range(1, Y):
        q_to_y(k).wait_send()
    q_to_sib.wait_send()
    for cp in fwd_copies:
        cp.wait_send()
    each(1, C, lambda k: l_copy(k).wait_send())
    for k in range(1, NQ):
        t_copy(k).wait_send()
    sh_copy.wait_send()
    for yy in range(Y):
        a_copy(yy).wait_send()
    for n in range(NC):
        for k in range(1, 2 * Y):
            b_copy(n, k)[1].wait_send()

        def c_done(k, n=n):
            to, cp = c_copy(n, k)
            when(full, to < nred, cp.wait_send)

        each(1, CZ, c_done)
        when(full, m < nred, lambda n=n: each(1, C, lambda k: f_copy(n, k).wait_send()))


def write_out(gq_in, gd_in, gq_out, gd_out, gq_sem, gd_sem):
    a = pltpu.make_async_copy(gd_in, gd_out, gd_sem)
    b = pltpu.make_async_copy(gq_in, gq_out, gq_sem)
    a.start()
    b.start()
    a.wait()
    b.wait()


def per_device(C, NQ, queries, documents, candidates):
    nq, qlen, width = queries.shape
    nd, tok, _ = documents.shape
    rows = nq * qlen
    Y = NQ // 2
    half = rows // 2
    rpc = max(16, rows // C)
    nred = half // rpc
    CZ = C // 2
    NC = 3 if width % 384 == 0 else 1
    cw = width // NC
    dma = pltpu.SemaphoreType.DMA
    V = pltpu.VMEM
    loss, gq, gd = pl.pallas_call(
        functools.partial(kernel, C, NQ, qlen),
        out_shape=(
            jax.ShapeDtypeStruct((1, 1), f32),
            pltpu.VMEM((rows, width), bf16),
            pltpu.VMEM((nd, tok, width), bf16),
        ),
        in_specs=[
            pl.BlockSpec(memory_space=pltpu.HBM),
            pl.BlockSpec(memory_space=pltpu.HBM),
            pl.BlockSpec(memory_space=pltpu.HBM),
        ],
        out_specs=(
            pl.BlockSpec(memory_space=pltpu.SMEM),
            pl.BlockSpec(memory_space=pltpu.VMEM),
            pl.BlockSpec(memory_space=pltpu.VMEM),
        ),
        scratch_shapes=[
            V((NQ, rows, width), bf16),
            V((nd, tok, width), bf16),
            V((NQ, nd, tok, rows), f32),
            V((nd, NQ, rows, width), f32),
            V((nd * NQ, rows), f32),
            V((nd * NQ, rows), f32),
            V((C, nd * NQ, rows), f32),
            V((NQ, nd * NQ, rows), f32),
            V((nd * NQ, rows), f32),
            V((nd * NQ, rows), f32),
            V((nd * NQ, rows), f32),
            V((nd * NQ, rows), f32),
            V((Y, 2 * nd, rows, 128), f32),
            V((Y, nd, rows, width), bf16),
            V((Y, nd, rows, width), bf16),
            V((NC, 2 * Y, half, cw), bf16),
            V((NC, 2 * Y, half, cw), bf16),
            V((NC, half, cw), f32),
            V((NC, nred, rpc, cw), bf16),
            V((NC, CZ, rpc, cw), bf16),
            V((NC, rpc, cw), bf16),
            V((NC, 2, nred, rpc, cw), bf16),
            pltpu.SMEM(candidates.shape[::-1], jnp.int32),
            dma((nd,)), dma, dma,
            dma((Y,)), dma((NQ,)), dma((Y,)),
            dma((C,)), dma((C,)),
            dma((NQ,)), dma((NQ,)), dma((2,)),
            dma((Y,)), dma((Y,)),
            dma((NC, 2 * Y)), dma((NC, 2 * Y)),
            dma((NC, CZ)), dma((NC, CZ)),
            dma((NC, C)), dma((NC, C)),
        ],
        compiler_params=pltpu.CompilerParams(
            collective_id=0, has_side_effects=True, vmem_limit_bytes=48 * 1024 * 1024),
    )(
        pltpu.with_memory_space_constraint(jnp.transpose(candidates), pltpu.HBM),
        pltpu.with_memory_space_constraint(queries.reshape(rows, width), pltpu.HBM),
        pltpu.with_memory_space_constraint(documents, pltpu.HBM),
    )
    gq, gd = pl.pallas_call(
        write_out,
        out_shape=(
            jax.ShapeDtypeStruct((rows, width), bf16),
            jax.ShapeDtypeStruct((nd, tok, width), bf16),
        ),
        in_specs=[pl.BlockSpec(memory_space=pl.ANY)] * 2,
        out_specs=(pl.BlockSpec(memory_space=pl.ANY),) * 2,
        scratch_shapes=[dma, dma],
    )(
        pltpu.with_memory_space_constraint(gq, pltpu.VMEM),
        pltpu.with_memory_space_constraint(gd, pltpu.VMEM),
    )
    return loss.reshape(()), gq.reshape(nq, qlen, width), gd


def solution(mesh):
    return jax.shard_map(
        functools.partial(per_device, mesh.shape["ctx"], mesh.shape["qg"]),
        mesh=mesh,
        in_specs=(P("qg", None, None), P("qg", "ctx", None), P()),
        out_specs=(P(), P("qg", None, None), P("qg", "ctx", None)),
        check_vma=False,
    )
```

```python
import functools

import jax
import jax.numpy as jnp
from jax import lax
from jax.experimental import pallas as pl
from jax.experimental.pallas import tpu as pltpu
from jax.sharding import PartitionSpec as P

sharpness_factor = 2.0
loss_scale = 1024.0
MESH = pl.DeviceIdType.MESH
f32 = jnp.float32
bf16 = jnp.bfloat16


def each(lo, hi, f):
    if hi - lo <= 16:
        for k in range(lo, hi):
            f(k)
    else:
        pl.loop(lo, hi)(f)


def when(always, cond, f):
    if always:
        f()
    else:
        pl.when(cond)(f)


def wrap(i, n):
    return lax.rem(i + 2 * n, n)


def kernel(
    C, NQ, qlen,
    cand_hbm, q_hbm, d_hbm,
    loss_ref, gq_ref, gd,
    Q, D, E, G, M, L, Lr, T, S, Sh, Shr, Ss, SC, As, Ar, Bs, Br, Mine, Cs, Cr, Fs, Fr, cand,
    d_sem, ql, cand_sem, qs, qr, fs, ls, lr, ts, tr, sh_sem, a_s, a_r, b_s, b_r, c_s, c_r, f_s, f_r,
):
    nd, tok, width = D.shape
    rows = Q.shape[1]
    Y = NQ // 2
    nq = rows // qlen
    slots = cand.shape[0]
    NC = Mine.shape[0]
    cw = width // NC
    rpc = Cr.shape[2]
    half = rows // 2
    nred = half // rpc
    CZ = C // 2
    full = nred == CZ
    c = lax.axis_index("ctx")
    g = lax.axis_index("qg")
    m = c // 2
    b = lax.rem(c, 2)
    y = g // 2
    core = lax.rem(g, 2)
    sib = 2 * y + 1 - core

    def rc(src, dst, ssem, rsem, cc, gg):
        return pltpu.make_async_remote_copy(
            src_ref=src, dst_ref=dst, send_sem=ssem, recv_sem=rsem,
            device_id=(cc, gg), device_id_type=MESH,
        )

    barrier = pltpu.get_barrier_semaphore()
    for k in range(1, NQ):
        pl.semaphore_signal(barrier, inc=1, device_id=(c, wrap(g + k, NQ)), device_id_type=MESH)
    each(1, C, lambda k: pl.semaphore_signal(
        barrier, inc=1, device_id=(wrap(c + k, C), g), device_id_type=MESH))
    for k in range(1, Y):
        pl.semaphore_signal(
            barrier, inc=1, device_id=(2 * m + 1 - b, wrap(g + 2 * k, NQ)), device_id_type=MESH)
    q_own = pltpu.make_async_copy(q_hbm, Q.at[g], ql)
    q_own.start()
    cand_copy = pltpu.make_async_copy(cand_hbm, cand, cand_sem)
    cand_copy.start()
    dcopy = [pltpu.make_async_copy(d_hbm.at[d], D.at[d], d_sem.at[d]) for d in range(nd)]
    for x in dcopy:
        x.start()
    pl.semaphore_wait(barrier, NQ - 1 + C - 1 + Y - 1)

    def q_to_y(k):
        return rc(q_hbm, Q.at[g], qs.at[k], qr.at[g], c, wrap(g + 2 * k, NQ))

    q_to_sib = rc(q_hbm, Q.at[g], qs.at[0], qr.at[g], c, sib)
    for k in range(1, Y):
        q_to_y(k).start()
    q_to_sib.start()

    lane_q = lax.broadcasted_iota(jnp.int32, (NQ, rows), 1) // qlen
    sub_g = lax.broadcasted_iota(jnp.int32, (NQ, rows), 0)
    qid = sub_g * nq + lane_q
    ids = []
    cand_copy.wait()
    for k in range(slots):
        v = jnp.zeros((NQ, rows), jnp.int32)
        for q in range(cand.shape[1]):
            v = jnp.where(qid == q, cand[k, q], v)
        ids.append(v)

    def wait_q(src):
        rc(q_hbm, Q.at[src], qs.at[0], qr.at[src], c, sib).wait_recv()

    def fwd(first, n):
        qb = Q[pl.ds(first, n)].reshape(n * rows, width)
        for d in range(nd):
            lg = sharpness_factor * lax.dot_general(
                D[d], qb, (((1,), (1,)), ((), ())), preferred_element_type=f32)
            m = jnp.max(lg, axis=0, keepdims=True)
            e = jnp.exp(lg - m)
            lp = m + jnp.log(jnp.sum(e, axis=0, keepdims=True))
            for h in range(n):
                r = pl.ds(d * NQ + first + h, 1)
                E[first + h, d] = e[:, h * rows:(h + 1) * rows]
                M[r, :] = m[:, h * rows:(h + 1) * rows]
                L[r, :] = lp[:, h * rows:(h + 1) * rows]

    def a_copy(yb):
        return rc(As.at[yb], Ar.at[yb], a_s.at[yb], a_r.at[yb], c, sib)

    def gmat(yb):
        for d in range(nd):
            e = jnp.concatenate([E[2 * yb, d].astype(bf16), E[2 * yb + 1, d].astype(bf16)], axis=1)
            p = lax.dot_general(
                e, D[d], (((0,), (0,)), ((), ())), preferred_element_type=f32)
            G[d, pl.ds(2 * yb, 2)] = p.reshape(2, rows, width)
            As[yb, d] = G[d, 2 * yb + 1 - core].astype(bf16)
        a_copy(yb).start()

    q_own.wait()
    wait_q(sib)
    for x in dcopy:
        x.wait()
    fwd(2 * y, 2)
    gmat(y)
    fwd_copies = []
    for k in range(1, Y):
        src = wrap(g - 2 * k, NQ)
        wait_q(src)
        cp = rc(Q.at[src], Q.at[src], fs.at[k], qr.at[src], c, sib)
        cp.start()
        fwd_copies.append(cp)
        fwd(src, 1)
    for k in range(1, Y):
        src = wrap(sib - 2 * k, NQ)
        wait_q(src)
        fwd(src, 1)

    def l_copy(k):
        return rc(L, Lr.at[k], ls.at[k], lr.at[k], wrap(c + k, C), g)

    each(1, C, lambda k: l_copy(k).start())
    for k in range(1, Y):
        gmat(wrap(y - k, Y))
    Lr[0] = L[...]
    each(1, C, lambda k: l_copy(k).wait_recv())
    parts = Lr[...]
    top = jnp.max(parts, axis=0)
    lse = top + jnp.log(jnp.sum(jnp.exp(parts - top[None]), axis=0))

    same = (lax.broadcasted_iota(jnp.int32, (rows, rows), 0) // qlen
            == lax.broadcasted_iota(jnp.int32, (rows, rows), 1) // qlen).astype(f32)
    T[g] = lax.dot_general(
        lse, same, (((1,), (0,)), ((), ())),
        precision=lax.Precision.HIGHEST, preferred_element_type=f32) / sharpness_factor

    def t_copy(k):
        return rc(T.at[g], T.at[g], ts.at[k], tr.at[k], c, wrap(g + k, NQ))

    for k in range(1, NQ):
        t_copy(k).start()
    Sh[...] = jnp.exp(M[...] - lse)
    sh_copy = rc(Sh, Shr, sh_sem.at[0], sh_sem.at[1], c, sib)
    sh_copy.start()
    for k in range(1, NQ):
        src = wrap(g - k, NQ)
        rc(T.at[src], T.at[src], ts.at[k], tr.at[k], c, src).wait_recv()

    pairs = []
    for k in range(slots):
        v = jnp.zeros((NQ, rows), f32)
        for gg in range(NQ):
            for d in range(nd):
                v = jnp.where(ids[k] == gg * nd + d, T[gg, d * NQ:(d + 1) * NQ, :], v)
        pairs.append(v)
    highest = functools.reduce(jnp.maximum, pairs)
    total = highest + jnp.log(functools.reduce(jnp.add, [jnp.exp(p - highest) for p in pairs]))
    loss_ref[0, 0] = jnp.sum(total - pairs[0]) / (NQ * rows)
    dz = [
        loss_scale / (NQ * nq) * (jnp.exp(p - total) - (1.0 if k == 0 else 0.0))
        for k, p in enumerate(pairs)
    ]
    sh_copy.wait_recv()
    for d in range(nd):
        r = slice(d * NQ, (d + 1) * NQ)
        for grp, shrink, dst in ((g, Sh, S), (sib, Shr, Ss)):
            w = jnp.zeros((NQ, rows), f32)
            for k in range(slots):
                w = w + jnp.where(ids[k] == grp * nd + d, dz[k], 0.0)
            dst[r, :] = w * shrink[r, :]
    own = [
        src[pl.ds(d * NQ + 2 * yy + core, 1), :]
        for yy in range(Y) for src in (S, Ss) for d in range(nd)
    ]
    St = jnp.transpose(jnp.concatenate(own, axis=0))
    for i in range(len(own)):
        SC[i // (2 * nd), i % (2 * nd)] = jnp.broadcast_to(St[:, i:i + 1], (rows, 128))

    for k in range(Y):
        a_copy(wrap(y - k, Y)).wait_recv()

    def scaled(yy, h, lo):
        at = slice(lo, lo + 128)
        r = pl.ds(pl.multiple_of(h * half, half), half)
        v = SC[yy, 0, r, :] * G[0, 2 * yy + core, r, at]
        for d in range(1, nd):
            v = v + SC[yy, d, r, :] * G[d, 2 * yy + core, r, at]
        for d in range(nd):
            v = v + SC[yy, nd + d, r, :] * Ar[yy, d, r, at].astype(f32)
        return v

    u = 2 * y + b

    def b_copy(n, k):
        to = wrap(u + k, 2 * Y)
        return to, rc(Bs.at[n, k], Br.at[n, k], b_s.at[n, k], b_r.at[n, k],
                      2 * m + lax.rem(to, 2), 2 * (to // 2) + core)

    for n in range(NC):
        for k in range(1, 2 * Y):
            to, cp = b_copy(n, k)
            for lo in range(0, cw, 128):
                Bs[n, k, :, lo:lo + 128] = scaled(
                    to // 2, lax.rem(to, 2), n * cw + lo).astype(bf16)
            cp.start()
    for n in range(NC):
        for lo in range(0, cw, 128):
            Mine[n, :, lo:lo + 128] = scaled(y, b, n * cw + lo)

    def doc_grad(d):
        acc = None
        for yb in range(Y):
            r = d * NQ + 2 * yb
            wt = jnp.concatenate(
                [(E[2 * yb + h, d] * S[r + h:r + h + 1, :]).astype(bf16) for h in range(2)], axis=1)
            part = jnp.dot(wt, Q[2 * yb:2 * yb + 2].reshape(2 * rows, width),
                           preferred_element_type=f32)
            acc = part if acc is None else acc + part
        gd[d] = acc.astype(bf16)

    for d in range(nd // 2):
        doc_grad(d)

    share = lax.rem(m, nred)

    def c_copy(n, k):
        to = wrap(m + k, CZ)
        return to, rc(
            Cs.at[n, lax.rem(to, nred)], Cr.at[n, k], c_s.at[n, k], c_r.at[n, k], 2 * to + b, g)

    def f_copy(n, k):
        return rc(Fs.at[n], Fr.at[n, b, share], f_s.at[n, k], f_r.at[n, k], wrap(c + k, C), g)

    for n in range(NC):
        for k in range(1, 2 * Y):
            b_copy(n, k)[1].wait_recv()
            Mine[n] = Mine[n] + Br[n, k].astype(f32)
        Cs[n] = Mine[n].astype(bf16).reshape(nred, rpc, cw)

        def c_start(k, n=n):
            to, cp = c_copy(n, k)
            when(full, to < nred, cp.start)

        each(1, CZ, c_start)

    for n in range(NC):
        def reduce_share(n=n):
            at = pl.multiple_of(share * rpc, rpc)
            Cr[n, 0] = jnp.zeros((rpc, cw), bf16)
            each(1, CZ, lambda k: c_copy(n, k)[1].wait_recv())
            v = Mine[n, pl.ds(at, rpc), :] + jnp.sum(Cr[n].astype(f32), axis=0)
            Fs[n] = v.astype(bf16)
            each(1, C, lambda k: f_copy(n, k).start())
            Fr[n, b, share] = Fs[n]

        when(full, m < nred, reduce_share)

    for d in range(nd // 2, nd):
        doc_grad(d)

    for n in range(NC):
        def f_wait(k, n=n):
            src = wrap(c - k, C)
            cp = rc(Fs.at[n], Fr.at[n, lax.rem(src, 2), lax.rem(src // 2, nred)],
                    f_s.at[n, k], f_r.at[n, k], src, g)
            when(full, src // 2 < nred, cp.wait_recv)

        each(1, C, f_wait)
        gq_ref[:, n * cw:(n + 1) * cw] = Fr[n].reshape(rows, cw)

    for k in range(1, Y):
        q_to_y(k).wait_send()
    q_to_sib.wait_send()
    for cp in fwd_copies:
        cp.wait_send()
    each(1, C, lambda k: l_copy(k).wait_send())
    for k in range(1, NQ):
        t_copy(k).wait_send()
    sh_copy.wait_send()
    for yy in range(Y):
        a_copy(yy).wait_send()
    for n in range(NC):
        for k in range(1, 2 * Y):
            b_copy(n, k)[1].wait_send()

        def c_done(k, n=n):
            to, cp = c_copy(n, k)
            when(full, to < nred, cp.wait_send)

        each(1, CZ, c_done)
        when(full, m < nred, lambda n=n: each(1, C, lambda k: f_copy(n, k).wait_send()))


def write_out(gq_in, gd_in, gq_out, gd_out, gq_sem, gd_sem):
    a = pltpu.make_async_copy(gd_in, gd_out, gd_sem)
    b = pltpu.make_async_copy(gq_in, gq_out, gq_sem)
    a.start()
    b.start()
    a.wait()
    b.wait()


def per_device(C, NQ, queries, documents, candidates):
    nq, qlen, width = queries.shape
    nd, tok, _ = documents.shape
    rows = nq * qlen
    Y = NQ // 2
    half = rows // 2
    rpc = max(16, rows // C)
    nred = half // rpc
    CZ = C // 2
    NC = 3 if width % 384 == 0 else 1
    cw = width // NC
    dma = pltpu.SemaphoreType.DMA
    V = pltpu.VMEM
    loss, gq, gd = pl.pallas_call(
        functools.partial(kernel, C, NQ, qlen),
        out_shape=(
            jax.ShapeDtypeStruct((1, 1), f32),
            pltpu.VMEM((rows, width), bf16),
            pltpu.VMEM((nd, tok, width), bf16),
        ),
        in_specs=[
            pl.BlockSpec(memory_space=pltpu.HBM),
            pl.BlockSpec(memory_space=pltpu.HBM),
            pl.BlockSpec(memory_space=pltpu.HBM),
        ],
        out_specs=(
            pl.BlockSpec(memory_space=pltpu.SMEM),
            pl.BlockSpec(memory_space=pltpu.VMEM),
            pl.BlockSpec(memory_space=pltpu.VMEM),
        ),
        scratch_shapes=[
            V((NQ, rows, width), bf16),
            V((nd, tok, width), bf16),
            V((NQ, nd, tok, rows), f32),
            V((nd, NQ, rows, width), f32),
            V((nd * NQ, rows), f32),
            V((nd * NQ, rows), f32),
            V((C, nd * NQ, rows), f32),
            V((NQ, nd * NQ, rows), f32),
            V((nd * NQ, rows), f32),
            V((nd * NQ, rows), f32),
            V((nd * NQ, rows), f32),
            V((nd * NQ, rows), f32),
            V((Y, 2 * nd, rows, 128), f32),
            V((Y, nd, rows, width), bf16),
            V((Y, nd, rows, width), bf16),
            V((NC, 2 * Y, half, cw), bf16),
            V((NC, 2 * Y, half, cw), bf16),
            V((NC, half, cw), f32),
            V((NC, nred, rpc, cw), bf16),
            V((NC, CZ, rpc, cw), bf16),
            V((NC, rpc, cw), bf16),
            V((NC, 2, nred, rpc, cw), bf16),
            pltpu.SMEM(candidates.shape[::-1], jnp.int32),
            dma((nd,)), dma, dma,
            dma((Y,)), dma((NQ,)), dma((Y,)),
            dma((C,)), dma((C,)),
            dma((NQ,)), dma((NQ,)), dma((2,)),
            dma((Y,)), dma((Y,)),
            dma((NC, 2 * Y)), dma((NC, 2 * Y)),
            dma((NC, CZ)), dma((NC, CZ)),
            dma((NC, C)), dma((NC, C)),
        ],
        compiler_params=pltpu.CompilerParams(
            collective_id=0, has_side_effects=True, vmem_limit_bytes=48 * 1024 * 1024),
    )(
        pltpu.with_memory_space_constraint(jnp.transpose(candidates), pltpu.HBM),
        pltpu.with_memory_space_constraint(queries.reshape(rows, width), pltpu.HBM),
        pltpu.with_memory_space_constraint(documents, pltpu.HBM),
    )
    gq, gd = pl.pallas_call(
        write_out,
        out_shape=(
            jax.ShapeDtypeStruct((rows, width), bf16),
            jax.ShapeDtypeStruct((nd, tok, width), bf16),
        ),
        in_specs=[pl.BlockSpec(memory_space=pl.ANY)] * 2,
        out_specs=(pl.BlockSpec(memory_space=pl.ANY),) * 2,
        scratch_shapes=[dma, dma],
    )(
        pltpu.with_memory_space_constraint(gq, pltpu.VMEM),
        pltpu.with_memory_space_constraint(gd, pltpu.VMEM),
    )
    return loss.reshape(()), gq.reshape(nq, qlen, width), gd


def solution(mesh):
    return jax.shard_map(
        functools.partial(per_device, mesh.shape["ctx"], mesh.shape["qg"]),
        mesh=mesh,
        in_specs=(P("qg", None, None), P("qg", "ctx", None), P()),
        out_specs=(P(), P("qg", None, None), P("qg", "ctx", None)),
        check_vma=False,
    )
```

```python
import functools

import jax
import jax.numpy as jnp
from jax import lax
from jax.experimental import pallas as pl
from jax.experimental.pallas import tpu as pltpu
from jax.sharding import PartitionSpec as P

sharpness_factor = 2.0
loss_scale = 1024.0
MESH = pl.DeviceIdType.MESH
f32 = jnp.float32
bf16 = jnp.bfloat16


def each(lo, hi, f):
    if hi - lo <= 16:
        for k in range(lo, hi):
            f(k)
    else:
        pl.loop(lo, hi)(f)


def when(always, cond, f):
    if always:
        f()
    else:
        pl.when(cond)(f)


def wrap(i, n):
    return lax.rem(i + 2 * n, n)


def kernel(
    C, NQ, qlen,
    cand_hbm, q_hbm, d_hbm,
    loss_ref, gq_ref, gd,
    Q, D, E, G, M, L, Lr, T, S, Sh, Shr, Ss, SC, As, Ar, Bs, Br, Mine, Cs, Cr, Fs, Fr, cand,
    d_sem, ql, cand_sem, qs, qr, fs, ls, lr, ts, tr, sh_sem, a_s, a_r, b_s, b_r, c_s, c_r, f_s, f_r,
):
    nd, tok, width = D.shape
    rows = Q.shape[1]
    Y = NQ // 2
    nq = rows // qlen
    slots = cand.shape[0]
    NC = Mine.shape[0]
    cw = width // NC
    rpc = Cr.shape[2]
    half = rows // 2
    nred = half // rpc
    CZ = C // 2
    full = nred == CZ
    c = lax.axis_index("ctx")
    g = lax.axis_index("qg")
    m = c // 2
    b = lax.rem(c, 2)
    y = g // 2
    core = lax.rem(g, 2)
    sib = 2 * y + 1 - core

    def rc(src, dst, ssem, rsem, cc, gg):
        return pltpu.make_async_remote_copy(
            src_ref=src, dst_ref=dst, send_sem=ssem, recv_sem=rsem,
            device_id=(cc, gg), device_id_type=MESH,
        )

    barrier = pltpu.get_barrier_semaphore()
    for k in range(1, NQ):
        pl.semaphore_signal(barrier, inc=1, device_id=(c, wrap(g + k, NQ)), device_id_type=MESH)
    each(1, C, lambda k: pl.semaphore_signal(
        barrier, inc=1, device_id=(wrap(c + k, C), g), device_id_type=MESH))
    for k in range(1, Y):
        pl.semaphore_signal(
            barrier, inc=1, device_id=(2 * m + 1 - b, wrap(g + 2 * k, NQ)), device_id_type=MESH)
    q_own = pltpu.make_async_copy(q_hbm, Q.at[g], ql)
    q_own.start()
    cand_copy = pltpu.make_async_copy(cand_hbm, cand, cand_sem)
    cand_copy.start()
    dcopy = [pltpu.make_async_copy(d_hbm.at[d], D.at[d], d_sem.at[d]) for d in range(nd)]
    for x in dcopy:
        x.start()
    pl.semaphore_wait(barrier, NQ - 1 + C - 1 + Y - 1)

    def q_to_y(k):
        return rc(q_hbm, Q.at[g], qs.at[k], qr.at[g], c, wrap(g + 2 * k, NQ))

    q_to_sib = rc(q_hbm, Q.at[g], qs.at[0], qr.at[g], c, sib)
    for k in range(1, Y):
        q_to_y(k).start()
    q_to_sib.start()

    lane_q = lax.broadcasted_iota(jnp.int32, (NQ, rows), 1) // qlen
    sub_g = lax.broadcasted_iota(jnp.int32, (NQ, rows), 0)
    qid = sub_g * nq + lane_q
    ids = []
    cand_copy.wait()
    for k in range(slots):
        v = jnp.zeros((NQ, rows), jnp.int32)
        for q in range(cand.shape[1]):
            v = jnp.where(qid == q, cand[k, q], v)
        ids.append(v)

    def wait_q(src):
        rc(q_hbm, Q.at[src], qs.at[0], qr.at[src], c, sib).wait_recv()

    def fwd(first, n):
        qb = Q[pl.ds(first, n)].reshape(n * rows, width)
        for d in range(nd):
            lg = sharpness_factor * lax.dot_general(
                D[d], qb, (((1,), (1,)), ((), ())), preferred_element_type=f32)
            m = jnp.max(lg, axis=0, keepdims=True)
            e = jnp.exp(lg - m)
            lp = m + jnp.log(jnp.sum(e, axis=0, keepdims=True))
            for h in range(n):
                r = pl.ds(d * NQ + first + h, 1)
                E[first + h, d] = e[:, h * rows:(h + 1) * rows]
                M[r, :] = m[:, h * rows:(h + 1) * rows]
                L[r, :] = lp[:, h * rows:(h + 1) * rows]

    def a_copy(yb):
        return rc(As.at[yb], Ar.at[yb], a_s.at[yb], a_r.at[yb], c, sib)

    def gmat(yb, docs, last):
        for d in docs:
            e = jnp.concatenate([E[2 * yb, d].astype(bf16), E[2 * yb + 1, d].astype(bf16)], axis=1)
            p = lax.dot_general(
                e, D[d], (((0,), (0,)), ((), ())), preferred_element_type=f32)
            G[d, pl.ds(2 * yb, 2)] = p.reshape(2, rows, width)
            As[yb, d] = G[d, 2 * yb + 1 - core].astype(bf16)
        if last:
            a_copy(yb).start()

    q_own.wait()
    wait_q(sib)
    for x in dcopy:
        x.wait()
    fwd(2 * y, 2)
    gmat(y, range(nd // 2), False)
    fwd_copies = []
    for k in range(1, Y):
        src = wrap(g - 2 * k, NQ)
        wait_q(src)
        cp = rc(Q.at[src], Q.at[src], fs.at[k], qr.at[src], c, sib)
        cp.start()
        fwd_copies.append(cp)
        fwd(src, 1)
    gmat(y, range(nd // 2, nd), True)
    for k in range(1, Y):
        src = wrap(sib - 2 * k, NQ)
        wait_q(src)
        fwd(src, 1)

    def l_copy(k):
        return rc(L, Lr.at[k], ls.at[k], lr.at[k], wrap(c + k, C), g)

    each(1, C, lambda k: l_copy(k).start())
    for k in range(1, Y):
        gmat(wrap(y - k, Y), range(nd), True)
    Lr[0] = L[...]
    each(1, C, lambda k: l_copy(k).wait_recv())
    parts = Lr[...]
    top = jnp.max(parts, axis=0)
    lse = top + jnp.log(jnp.sum(jnp.exp(parts - top[None]), axis=0))

    same = (lax.broadcasted_iota(jnp.int32, (rows, rows), 0) // qlen
            == lax.broadcasted_iota(jnp.int32, (rows, rows), 1) // qlen).astype(f32)
    T[g] = lax.dot_general(
        lse, same, (((1,), (0,)), ((), ())),
        precision=lax.Precision.HIGHEST, preferred_element_type=f32) / sharpness_factor

    def t_copy(k):
        return rc(T.at[g], T.at[g], ts.at[k], tr.at[k], c, wrap(g + k, NQ))

    for k in range(1, NQ):
        t_copy(k).start()
    Sh[...] = jnp.exp(M[...] - lse)
    sh_copy = rc(Sh, Shr, sh_sem.at[0], sh_sem.at[1], c, sib)
    sh_copy.start()
    for k in range(1, NQ):
        src = wrap(g - k, NQ)
        rc(T.at[src], T.at[src], ts.at[k], tr.at[k], c, src).wait_recv()

    pairs = []
    for k in range(slots):
        v = jnp.zeros((NQ, rows), f32)
        for gg in range(NQ):
            for d in range(nd):
                v = jnp.where(ids[k] == gg * nd + d, T[gg, d * NQ:(d + 1) * NQ, :], v)
        pairs.append(v)
    highest = functools.reduce(jnp.maximum, pairs)
    total = highest + jnp.log(functools.reduce(jnp.add, [jnp.exp(p - highest) for p in pairs]))
    loss_ref[0, 0] = jnp.sum(total - pairs[0]) / (NQ * rows)
    dz = [
        loss_scale / (NQ * nq) * (jnp.exp(p - total) - (1.0 if k == 0 else 0.0))
        for k, p in enumerate(pairs)
    ]
    sh_copy.wait_recv()
    for d in range(nd):
        r = slice(d * NQ, (d + 1) * NQ)
        for grp, shrink, dst in ((g, Sh, S), (sib, Shr, Ss)):
            w = jnp.zeros((NQ, rows), f32)
            for k in range(slots):
                w = w + jnp.where(ids[k] == grp * nd + d, dz[k], 0.0)
            dst[r, :] = w * shrink[r, :]
    own = [
        src[pl.ds(d * NQ + 2 * yy + core, 1), :]
        for yy in range(Y) for src in (S, Ss) for d in range(nd)
    ]
    St = jnp.transpose(jnp.concatenate(own, axis=0))
    for i in range(len(own)):
        SC[i // (2 * nd), i % (2 * nd)] = jnp.broadcast_to(St[:, i:i + 1], (rows, 128))

    for k in range(Y):
        a_copy(wrap(y - k, Y)).wait_recv()

    def scaled(yy, h, lo):
        at = slice(lo, lo + 128)
        r = pl.ds(pl.multiple_of(h * half, half), half)
        v = SC[yy, 0, r, :] * G[0, 2 * yy + core, r, at]
        for d in range(1, nd):
            v = v + SC[yy, d, r, :] * G[d, 2 * yy + core, r, at]
        for d in range(nd):
            v = v + SC[yy, nd + d, r, :] * Ar[yy, d, r, at].astype(f32)
        return v

    u = 2 * y + b

    def b_copy(n, k):
        to = wrap(u + k, 2 * Y)
        return to, rc(Bs.at[n, k], Br.at[n, k], b_s.at[n, k], b_r.at[n, k],
                      2 * m + lax.rem(to, 2), 2 * (to // 2) + core)

    for n in range(NC):
        for k in range(1, 2 * Y):
            to, cp = b_copy(n, k)
            for lo in range(0, cw, 128):
                Bs[n, k, :, lo:lo + 128] = scaled(
                    to // 2, lax.rem(to, 2), n * cw + lo).astype(bf16)
            cp.start()
    for n in range(NC):
        for lo in range(0, cw, 128):
            Mine[n, :, lo:lo + 128] = scaled(y, b, n * cw + lo)

    def doc_grad(d):
        acc = None
        for yb in range(Y):
            r = d * NQ + 2 * yb
            wt = jnp.concatenate(
                [(E[2 * yb + h, d] * S[r + h:r + h + 1, :]).astype(bf16) for h in range(2)], axis=1)
            part = jnp.dot(wt, Q[2 * yb:2 * yb + 2].reshape(2 * rows, width),
                           preferred_element_type=f32)
            acc = part if acc is None else acc + part
        gd[d] = acc.astype(bf16)

    for d in range(nd // 2):
        doc_grad(d)

    share = lax.rem(m, nred)

    def c_copy(n, k):
        to = wrap(m + k, CZ)
        return to, rc(
            Cs.at[n, lax.rem(to, nred)], Cr.at[n, k], c_s.at[n, k], c_r.at[n, k], 2 * to + b, g)

    def f_copy(n, k):
        return rc(Fs.at[n], Fr.at[n, b, share], f_s.at[n, k], f_r.at[n, k], wrap(c + k, C), g)

    for n in range(NC):
        for k in range(1, 2 * Y):
            b_copy(n, k)[1].wait_recv()
            Mine[n] = Mine[n] + Br[n, k].astype(f32)
        Cs[n] = Mine[n].astype(bf16).reshape(nred, rpc, cw)

        def c_start(k, n=n):
            to, cp = c_copy(n, k)
            when(full, to < nred, cp.start)

        each(1, CZ, c_start)

    for d in range(nd // 2, nd):
        doc_grad(d)

    for n in range(NC):
        def reduce_share(n=n):
            at = pl.multiple_of(share * rpc, rpc)
            Cr[n, 0] = jnp.zeros((rpc, cw), bf16)
            each(1, CZ, lambda k: c_copy(n, k)[1].wait_recv())
            v = Mine[n, pl.ds(at, rpc), :] + jnp.sum(Cr[n].astype(f32), axis=0)
            Fs[n] = v.astype(bf16)
            each(1, C, lambda k: f_copy(n, k).start())
            Fr[n, b, share] = Fs[n]

        when(full, m < nred, reduce_share)

    for n in range(NC):
        def f_wait(k, n=n):
            src = wrap(c - k, C)
            cp = rc(Fs.at[n], Fr.at[n, lax.rem(src, 2), lax.rem(src // 2, nred)],
                    f_s.at[n, k], f_r.at[n, k], src, g)
            when(full, src // 2 < nred, cp.wait_recv)

        each(1, C, f_wait)
        gq_ref[:, n * cw:(n + 1) * cw] = Fr[n].reshape(rows, cw)

    for k in range(1, Y):
        q_to_y(k).wait_send()
    q_to_sib.wait_send()
    for cp in fwd_copies:
        cp.wait_send()
    each(1, C, lambda k: l_copy(k).wait_send())
    for k in range(1, NQ):
        t_copy(k).wait_send()
    sh_copy.wait_send()
    for yy in range(Y):
        a_copy(yy).wait_send()
    for n in range(NC):
        for k in range(1, 2 * Y):
            b_copy(n, k)[1].wait_send()

        def c_done(k, n=n):
            to, cp = c_copy(n, k)
            when(full, to < nred, cp.wait_send)

        each(1, CZ, c_done)
        when(full, m < nred, lambda n=n: each(1, C, lambda k: f_copy(n, k).wait_send()))


def write_out(gq_in, gd_in, gq_out, gd_out, gq_sem, gd_sem):
    a = pltpu.make_async_copy(gd_in, gd_out, gd_sem)
    b = pltpu.make_async_copy(gq_in, gq_out, gq_sem)
    a.start()
    b.start()
    a.wait()
    b.wait()


def per_device(C, NQ, queries, documents, candidates):
    nq, qlen, width = queries.shape
    nd, tok, _ = documents.shape
    rows = nq * qlen
    Y = NQ // 2
    half = rows // 2
    rpc = max(16, rows // C)
    nred = half // rpc
    CZ = C // 2
    NC = 6 if width % 768 == 0 else 1
    cw = width // NC
    dma = pltpu.SemaphoreType.DMA
    V = pltpu.VMEM
    loss, gq, gd = pl.pallas_call(
        functools.partial(kernel, C, NQ, qlen),
        out_shape=(
            jax.ShapeDtypeStruct((1, 1), f32),
            pltpu.VMEM((rows, width), bf16),
            pltpu.VMEM((nd, tok, width), bf16),
        ),
        in_specs=[
            pl.BlockSpec(memory_space=pltpu.HBM),
            pl.BlockSpec(memory_space=pltpu.HBM),
            pl.BlockSpec(memory_space=pltpu.HBM),
        ],
        out_specs=(
            pl.BlockSpec(memory_space=pltpu.SMEM),
            pl.BlockSpec(memory_space=pltpu.VMEM),
            pl.BlockSpec(memory_space=pltpu.VMEM),
        ),
        scratch_shapes=[
            V((NQ, rows, width), bf16),
            V((nd, tok, width), bf16),
            V((NQ, nd, tok, rows), f32),
            V((nd, NQ, rows, width), f32),
            V((nd * NQ, rows), f32),
            V((nd * NQ, rows), f32),
            V((C, nd * NQ, rows), f32),
            V((NQ, nd * NQ, rows), f32),
            V((nd * NQ, rows), f32),
            V((nd * NQ, rows), f32),
            V((nd * NQ, rows), f32),
            V((nd * NQ, rows), f32),
            V((Y, 2 * nd, rows, 128), f32),
            V((Y, nd, rows, width), bf16),
            V((Y, nd, rows, width), bf16),
            V((NC, 2 * Y, half, cw), bf16),
            V((NC, 2 * Y, half, cw), bf16),
            V((NC, half, cw), f32),
            V((NC, nred, rpc, cw), bf16),
            V((NC, CZ, rpc, cw), bf16),
            V((NC, rpc, cw), bf16),
            V((NC, 2, nred, rpc, cw), bf16),
            pltpu.SMEM(candidates.shape[::-1], jnp.int32),
            dma((nd,)), dma, dma,
            dma((Y,)), dma((NQ,)), dma((Y,)),
            dma((C,)), dma((C,)),
            dma((NQ,)), dma((NQ,)), dma((2,)),
            dma((Y,)), dma((Y,)),
            dma((NC, 2 * Y)), dma((NC, 2 * Y)),
            dma((NC, CZ)), dma((NC, CZ)),
            dma((NC, C)), dma((NC, C)),
        ],
        compiler_params=pltpu.CompilerParams(
            collective_id=0, has_side_effects=True, vmem_limit_bytes=48 * 1024 * 1024),
    )(
        pltpu.with_memory_space_constraint(jnp.transpose(candidates), pltpu.HBM),
        pltpu.with_memory_space_constraint(queries.reshape(rows, width), pltpu.HBM),
        pltpu.with_memory_space_constraint(documents, pltpu.HBM),
    )
    gq, gd = pl.pallas_call(
        write_out,
        out_shape=(
            jax.ShapeDtypeStruct((rows, width), bf16),
            jax.ShapeDtypeStruct((nd, tok, width), bf16),
        ),
        in_specs=[pl.BlockSpec(memory_space=pl.ANY)] * 2,
        out_specs=(pl.BlockSpec(memory_space=pl.ANY),) * 2,
        scratch_shapes=[dma, dma],
    )(
        pltpu.with_memory_space_constraint(gq, pltpu.VMEM),
        pltpu.with_memory_space_constraint(gd, pltpu.VMEM),
    )
    return loss.reshape(()), gq.reshape(nq, qlen, width), gd


def solution(mesh):
    return jax.shard_map(
        functools.partial(per_device, mesh.shape["ctx"], mesh.shape["qg"]),
        mesh=mesh,
        in_specs=(P("qg", None, None), P("qg", "ctx", None), P()),
        out_specs=(P(), P("qg", None, None), P("qg", "ctx", None)),
        check_vma=False,
    )
```

```python
import functools

import jax
import jax.numpy as jnp
from jax import lax
from jax.experimental import pallas as pl
from jax.experimental.pallas import tpu as pltpu
from jax.sharding import PartitionSpec as P

sharpness_factor = 2.0
loss_scale = 1024.0
MESH = pl.DeviceIdType.MESH
f32 = jnp.float32
bf16 = jnp.bfloat16


def each(lo, hi, f):
    if hi - lo <= 16:
        for k in range(lo, hi):
            f(k)
    else:
        pl.loop(lo, hi)(f)


def when(always, cond, f):
    if always:
        f()
    else:
        pl.when(cond)(f)


def wrap(i, n):
    return lax.rem(i + 2 * n, n)


def kernel(
    C, NQ, qlen,
    cand_hbm, q_hbm, d_hbm,
    loss_ref, gq_ref, gd,
    Q, D, E, G, M, L, Lr, T, S, Sh, Shr, Ss, SC, As, Ar, Bs, Br, Mine, Cs, Cr, Fs, Fr, cand,
    d_sem, ql, cand_sem, qs, qr, fs, ls, lr, ts, tr, sh_sem, a_s, a_r, b_s, b_r, c_s, c_r, f_s, f_r,
):
    nd, tok, width = D.shape
    rows = Q.shape[1]
    Y = NQ // 2
    nq = rows // qlen
    slots = cand.shape[0]
    NC = Mine.shape[0]
    cw = width // NC
    rpc = Cr.shape[2]
    half = rows // 2
    nred = half // rpc
    CZ = C // 2
    full = nred == CZ
    c = lax.axis_index("ctx")
    g = lax.axis_index("qg")
    m = c // 2
    b = lax.rem(c, 2)
    y = g // 2
    core = lax.rem(g, 2)
    sib = 2 * y + 1 - core

    def rc(src, dst, ssem, rsem, cc, gg):
        return pltpu.make_async_remote_copy(
            src_ref=src, dst_ref=dst, send_sem=ssem, recv_sem=rsem,
            device_id=(cc, gg), device_id_type=MESH,
        )

    barrier = pltpu.get_barrier_semaphore()
    for k in range(1, NQ):
        pl.semaphore_signal(barrier, inc=1, device_id=(c, wrap(g + k, NQ)), device_id_type=MESH)
    each(1, C, lambda k: pl.semaphore_signal(
        barrier, inc=1, device_id=(wrap(c + k, C), g), device_id_type=MESH))
    for k in range(1, Y):
        pl.semaphore_signal(
            barrier, inc=1, device_id=(2 * m + 1 - b, wrap(g + 2 * k, NQ)), device_id_type=MESH)
    q_own = pltpu.make_async_copy(q_hbm, Q.at[g], ql)
    q_own.start()
    cand_copy = pltpu.make_async_copy(cand_hbm, cand, cand_sem)
    cand_copy.start()
    dcopy = [pltpu.make_async_copy(d_hbm.at[d], D.at[d], d_sem.at[d]) for d in range(nd)]
    for x in dcopy:
        x.start()
    pl.semaphore_wait(barrier, NQ - 1 + C - 1 + Y - 1)

    def q_to_y(k):
        return rc(q_hbm, Q.at[g], qs.at[k], qr.at[g], c, wrap(g + 2 * k, NQ))

    q_to_sib = rc(q_hbm, Q.at[g], qs.at[0], qr.at[g], c, sib)
    for k in range(1, Y):
        q_to_y(k).start()
    q_to_sib.start()

    lane_q = lax.broadcasted_iota(jnp.int32, (NQ, rows), 1) // qlen
    sub_g = lax.broadcasted_iota(jnp.int32, (NQ, rows), 0)
    qid = sub_g * nq + lane_q
    ids = []
    cand_copy.wait()
    for k in range(slots):
        v = jnp.zeros((NQ, rows), jnp.int32)
        for q in range(cand.shape[1]):
            v = jnp.where(qid == q, cand[k, q], v)
        ids.append(v)

    def wait_q(src):
        rc(q_hbm, Q.at[src], qs.at[0], qr.at[src], c, sib).wait_recv()

    def fwd(first, n):
        qb = Q[pl.ds(first, n)].reshape(n * rows, width)
        for d in range(nd):
            lg = sharpness_factor * lax.dot_general(
                D[d], qb, (((1,), (1,)), ((), ())), preferred_element_type=f32)
            m = jnp.max(lg, axis=0, keepdims=True)
            e = jnp.exp(lg - m)
            lp = m + jnp.log(jnp.sum(e, axis=0, keepdims=True))
            for h in range(n):
                r = pl.ds(d * NQ + first + h, 1)
                E[first + h, d] = e[:, h * rows:(h + 1) * rows]
                M[r, :] = m[:, h * rows:(h + 1) * rows]
                L[r, :] = lp[:, h * rows:(h + 1) * rows]

    def a_copy(yb):
        return rc(As.at[yb], Ar.at[yb], a_s.at[yb], a_r.at[yb], c, sib)

    def gmat(yb):
        for d in range(nd):
            e = jnp.concatenate([E[2 * yb, d].astype(bf16), E[2 * yb + 1, d].astype(bf16)], axis=1)
            p = lax.dot_general(
                e, D[d], (((0,), (0,)), ((), ())), preferred_element_type=f32)
            G[d, pl.ds(2 * yb, 2)] = p.reshape(2, rows, width)
            As[yb, d] = G[d, 2 * yb + 1 - core].astype(bf16)
        a_copy(yb).start()

    q_own.wait()
    wait_q(sib)
    for x in dcopy:
        x.wait()
    fwd(2 * y, 2)
    gmat(y)
    fwd_copies = []
    for k in range(1, Y):
        src = wrap(g - 2 * k, NQ)
        wait_q(src)
        cp = rc(Q.at[src], Q.at[src], fs.at[k], qr.at[src], c, sib)
        cp.start()
        fwd_copies.append(cp)
        fwd(src, 1)
    for k in range(1, Y):
        src = wrap(sib - 2 * k, NQ)
        wait_q(src)
        fwd(src, 1)

    def l_copy(k):
        return rc(L, Lr.at[k], ls.at[k], lr.at[k], wrap(c + k, C), g)

    each(1, C, lambda k: l_copy(k).start())
    for k in range(1, Y):
        gmat(wrap(y - k, Y))
    Lr[0] = L[...]
    each(1, C, lambda k: l_copy(k).wait_recv())
    parts = Lr[...]
    top = jnp.max(parts, axis=0)
    lse = top + jnp.log(jnp.sum(jnp.exp(parts - top[None]), axis=0))

    same = (lax.broadcasted_iota(jnp.int32, (rows, rows), 0) // qlen
            == lax.broadcasted_iota(jnp.int32, (rows, rows), 1) // qlen).astype(f32)
    T[g] = lax.dot_general(
        lse, same, (((1,), (0,)), ((), ())),
        precision=lax.Precision.HIGHEST, preferred_element_type=f32) / sharpness_factor

    def t_copy(k):
        return rc(T.at[g], T.at[g], ts.at[k], tr.at[k], c, wrap(g + k, NQ))

    for k in range(1, NQ):
        t_copy(k).start()
    Sh[...] = jnp.exp(M[...] - lse)
    sh_copy = rc(Sh, Shr, sh_sem.at[0], sh_sem.at[1], c, sib)
    sh_copy.start()
    for k in range(1, NQ):
        src = wrap(g - k, NQ)
        rc(T.at[src], T.at[src], ts.at[k], tr.at[k], c, src).wait_recv()

    pairs = []
    for k in range(slots):
        v = jnp.zeros((NQ, rows), f32)
        for gg in range(NQ):
            for d in range(nd):
                v = jnp.where(ids[k] == gg * nd + d, T[gg, d * NQ:(d + 1) * NQ, :], v)
        pairs.append(v)
    highest = functools.reduce(jnp.maximum, pairs)
    total = highest + jnp.log(functools.reduce(jnp.add, [jnp.exp(p - highest) for p in pairs]))
    loss_ref[0, 0] = jnp.sum(total - pairs[0]) / (NQ * rows)
    dz = [
        loss_scale / (NQ * nq) * (jnp.exp(p - total) - (1.0 if k == 0 else 0.0))
        for k, p in enumerate(pairs)
    ]
    sh_copy.wait_recv()
    for d in range(nd):
        r = slice(d * NQ, (d + 1) * NQ)
        for grp, shrink, dst in ((g, Sh, S), (sib, Shr, Ss)):
            w = jnp.zeros((NQ, rows), f32)
            for k in range(slots):
                w = w + jnp.where(ids[k] == grp * nd + d, dz[k], 0.0)
            dst[r, :] = w * shrink[r, :]
    own = [
        src[pl.ds(d * NQ + 2 * yy + core, 1), :]
        for yy in range(Y) for src in (S, Ss) for d in range(nd)
    ]
    St = jnp.transpose(jnp.concatenate(own, axis=0))
    for i in range(len(own)):
        SC[i // (2 * nd), i % (2 * nd)] = jnp.broadcast_to(St[:, i:i + 1], (rows, 128))

    for k in range(Y):
        a_copy(wrap(y - k, Y)).wait_recv()

    def scaled(yy, h, lo):
        at = slice(lo, lo + 128)
        r = pl.ds(pl.multiple_of(h * half, half), half)
        v = SC[yy, 0, r, :] * G[0, 2 * yy + core, r, at]
        for d in range(1, nd):
            v = v + SC[yy, d, r, :] * G[d, 2 * yy + core, r, at]
        for d in range(nd):
            v = v + SC[yy, nd + d, r, :] * Ar[yy, d, r, at].astype(f32)
        return v

    u = 2 * y + b

    def b_copy(n, k):
        to = wrap(u + k, 2 * Y)
        return to, rc(Bs.at[n, k], Br.at[n, k], b_s.at[n, k], b_r.at[n, k],
                      2 * m + lax.rem(to, 2), 2 * (to // 2) + core)

    for n in range(NC):
        for k in range(1, 2 * Y):
            to, cp = b_copy(n, k)
            for lo in range(0, cw, 128):
                Bs[n, k, :, lo:lo + 128] = scaled(
                    to // 2, lax.rem(to, 2), n * cw + lo).astype(bf16)
            cp.start()
    for n in range(NC):
        for lo in range(0, cw, 128):
            Mine[n, :, lo:lo + 128] = scaled(y, b, n * cw + lo)

    def doc_grad(d):
        acc = None
        for yb in range(Y):
            r = d * NQ + 2 * yb
            wt = jnp.concatenate(
                [(E[2 * yb + h, d] * S[r + h:r + h + 1, :]).astype(bf16) for h in range(2)], axis=1)
            part = jnp.dot(wt, Q[2 * yb:2 * yb + 2].reshape(2 * rows, width),
                           preferred_element_type=f32)
            acc = part if acc is None else acc + part
        gd[d] = acc.astype(bf16)

    for d in range(nd // 2):
        doc_grad(d)

    share = lax.rem(m, nred)

    def c_copy(n, k):
        to = wrap(m + k, CZ)
        return to, rc(
            Cs.at[n, lax.rem(to, nred)], Cr.at[n, k], c_s.at[n, k], c_r.at[n, k], 2 * to + b, g)

    def f_copy(n, k):
        return rc(Fs.at[n], Fr.at[n, b, share], f_s.at[n, k], f_r.at[n, k], wrap(c + k, C), g)

    for n in range(NC):
        for k in range(1, 2 * Y):
            b_copy(n, k)[1].wait_recv()
            Mine[n] = Mine[n] + Br[n, k].astype(f32)
        Cs[n] = Mine[n].astype(bf16).reshape(nred, rpc, cw)

        def c_start(k, n=n):
            to, cp = c_copy(n, k)
            when(full, to < nred, cp.start)

        each(1, CZ, c_start)

    for d in range(nd // 2, nd):
        doc_grad(d)

    for n in range(NC):
        def reduce_share(n=n):
            at = pl.multiple_of(share * rpc, rpc)
            Cr[n, 0] = jnp.zeros((rpc, cw), bf16)
            each(1, CZ, lambda k: c_copy(n, k)[1].wait_recv())
            v = Mine[n, pl.ds(at, rpc), :] + jnp.sum(Cr[n].astype(f32), axis=0)
            Fs[n] = v.astype(bf16)
            each(1, C, lambda k: f_copy(n, k).start())
            Fr[n, b, share] = Fs[n]

        when(full, m < nred, reduce_share)

    for n in range(NC):
        def f_wait(k, n=n):
            src = wrap(c - k, C)
            cp = rc(Fs.at[n], Fr.at[n, lax.rem(src, 2), lax.rem(src // 2, nred)],
                    f_s.at[n, k], f_r.at[n, k], src, g)
            when(full, src // 2 < nred, cp.wait_recv)

        each(1, C, f_wait)
        gq_ref[:, n * cw:(n + 1) * cw] = Fr[n].reshape(rows, cw)

    for k in range(1, Y):
        q_to_y(k).wait_send()
    q_to_sib.wait_send()
    for cp in fwd_copies:
        cp.wait_send()
    each(1, C, lambda k: l_copy(k).wait_send())
    for k in range(1, NQ):
        t_copy(k).wait_send()
    sh_copy.wait_send()
    for yy in range(Y):
        a_copy(yy).wait_send()
    for n in range(NC):
        for k in range(1, 2 * Y):
            b_copy(n, k)[1].wait_send()

        def c_done(k, n=n):
            to, cp = c_copy(n, k)
            when(full, to < nred, cp.wait_send)

        each(1, CZ, c_done)
        when(full, m < nred, lambda n=n: each(1, C, lambda k: f_copy(n, k).wait_send()))


def write_out(gq_in, gd_in, gq_out, gd_out, gq_sem, gd_sem):
    a = pltpu.make_async_copy(gd_in, gd_out, gd_sem)
    b = pltpu.make_async_copy(gq_in, gq_out, gq_sem)
    a.start()
    b.start()
    a.wait()
    b.wait()


def per_device(C, NQ, queries, documents, candidates):
    nq, qlen, width = queries.shape
    nd, tok, _ = documents.shape
    rows = nq * qlen
    Y = NQ // 2
    half = rows // 2
    rpc = max(16, rows // C)
    nred = half // rpc
    CZ = C // 2
    NC = 2 if width % 256 == 0 else 1
    cw = width // NC
    dma = pltpu.SemaphoreType.DMA
    V = pltpu.VMEM
    loss, gq, gd = pl.pallas_call(
        functools.partial(kernel, C, NQ, qlen),
        out_shape=(
            jax.ShapeDtypeStruct((1, 1), f32),
            pltpu.VMEM((rows, width), bf16),
            pltpu.VMEM((nd, tok, width), bf16),
        ),
        in_specs=[
            pl.BlockSpec(memory_space=pltpu.HBM),
            pl.BlockSpec(memory_space=pltpu.HBM),
            pl.BlockSpec(memory_space=pltpu.HBM),
        ],
        out_specs=(
            pl.BlockSpec(memory_space=pltpu.SMEM),
            pl.BlockSpec(memory_space=pltpu.VMEM),
            pl.BlockSpec(memory_space=pltpu.VMEM),
        ),
        scratch_shapes=[
            V((NQ, rows, width), bf16),
            V((nd, tok, width), bf16),
            V((NQ, nd, tok, rows), f32),
            V((nd, NQ, rows, width), f32),
            V((nd * NQ, rows), f32),
            V((nd * NQ, rows), f32),
            V((C, nd * NQ, rows), f32),
            V((NQ, nd * NQ, rows), f32),
            V((nd * NQ, rows), f32),
            V((nd * NQ, rows), f32),
            V((nd * NQ, rows), f32),
            V((nd * NQ, rows), f32),
            V((Y, 2 * nd, rows, 128), f32),
            V((Y, nd, rows, width), bf16),
            V((Y, nd, rows, width), bf16),
            V((NC, 2 * Y, half, cw), bf16),
            V((NC, 2 * Y, half, cw), bf16),
            V((NC, half, cw), f32),
            V((NC, nred, rpc, cw), bf16),
            V((NC, CZ, rpc, cw), bf16),
            V((NC, rpc, cw), bf16),
            V((NC, 2, nred, rpc, cw), bf16),
            pltpu.SMEM(candidates.shape[::-1], jnp.int32),
            dma((nd,)), dma, dma,
            dma((Y,)), dma((NQ,)), dma((Y,)),
            dma((C,)), dma((C,)),
            dma((NQ,)), dma((NQ,)), dma((2,)),
            dma((Y,)), dma((Y,)),
            dma((NC, 2 * Y)), dma((NC, 2 * Y)),
            dma((NC, CZ)), dma((NC, CZ)),
            dma((NC, C)), dma((NC, C)),
        ],
        compiler_params=pltpu.CompilerParams(
            collective_id=0, has_side_effects=True, vmem_limit_bytes=48 * 1024 * 1024),
    )(
        pltpu.with_memory_space_constraint(jnp.transpose(candidates), pltpu.HBM),
        pltpu.with_memory_space_constraint(queries.reshape(rows, width), pltpu.HBM),
        pltpu.with_memory_space_constraint(documents, pltpu.HBM),
    )
    gq, gd = pl.pallas_call(
        write_out,
        out_shape=(
            jax.ShapeDtypeStruct((rows, width), bf16),
            jax.ShapeDtypeStruct((nd, tok, width), bf16),
        ),
        in_specs=[pl.BlockSpec(memory_space=pl.ANY)] * 2,
        out_specs=(pl.BlockSpec(memory_space=pl.ANY),) * 2,
        scratch_shapes=[dma, dma],
    )(
        pltpu.with_memory_space_constraint(gq, pltpu.VMEM),
        pltpu.with_memory_space_constraint(gd, pltpu.VMEM),
    )
    return loss.reshape(()), gq.reshape(nq, qlen, width), gd


def solution(mesh):
    return jax.shard_map(
        functools.partial(per_device, mesh.shape["ctx"], mesh.shape["qg"]),
        mesh=mesh,
        in_specs=(P("qg", None, None), P("qg", "ctx", None), P()),
        out_specs=(P(), P("qg", None, None), P("qg", "ctx", None)),
        check_vma=False,
    )
```
